32 devices in a mesh: groups: 2 (over y), hold: 4 (over z), tp: 4 (over x, core).
Axes of the slice: x: 2, y: 2, z: 4, core: 2. Of those that a mesh axis runs over, the one named last changes fastest.
Arguments:
- cache_store: bfloat16 [2, 32, 256, 8, 2, 128], P(None, ('groups', 'hold'), None, 'tp'), parts along dimension 1, may hold values from -6 to 6
- span_lengths: int32 [8, 4], P(('groups', 'hold')), parts along dimension 0, may hold values from 1 to 256, 512 in all within a row
- span_holder: int32 [8, 4], P(('groups', 'hold')), parts along dimension 0, may hold values from 0 to 3, as said below
- rec_pos: int32 [2, 640], P(None, ('groups', 'hold')), parts along dimension 1, may hold values from 0 to 2047, as said below
- hidden: bfloat16 [2, 640, 12288], P(None, ('groups', 'hold')), parts along dimension 1, may hold values from -6 to 6
- norm_gain: bfloat16 [2, 12288], replicated, may hold values from 0.099609375 to 1.8984375
- kv_weight: bfloat16 [2, 12288, 8, 2, 128], P(None, 'hold', 'tp'), may hold values from -0.0546875 to 0.0546875
Outputs:
- united_cache: bfloat16 [2, 4096, 8, 2, 128], P(None, ('groups', 'hold'), 'tp'), parts along dimension 1
- deviation: float32 [2, 640], P(None, ('groups', 'hold')), parts along dimension 1
The draws below stay inside these ranges and needn't reach their ends.
There are 2 independent parts, one for each index of `groups`. The reference program is written for one: setup_inputs(seed, part) draws one part's arguments, and reference() takes and returns one part's arrays. A program takes and returns all parts, laid end to end along the dimension named above; an argument that names none is the same for every part. Nothing has to cross between parts.
Inputs may be any that keep to these rules, and one draw needn't show every extreme that they name: `span_holder`: each row holds 4 distinct holders. `rec_pos`: entries p * 80 to (p + 1) * 80 - 1 of each layer are distinct positions of block p in increasing order, the block's last position among them. `span_lengths`: each row sums to 512.
All inputs are finite; a program needn't handle non-finite values.
Results may differ from the reference program's by a relative error of at most 0.0019.
Values may be sent and summed in bfloat16 or wider, within the bound.
No kernel may reach another device: no remote copies, remote signals or barrier semaphores. Data moves between devices by JAX's collectives and lax.ppermute only.
A program may use at most 128 MiB of HBM per device.

```python
import math
import jax
import jax.numpy as jnp
import numpy as np
from jax import lax

D = 12288
KVH = 8
HD = 128
PROMPT_PER_HOLD = 512
LAYERS = 2
SPANS_PER_BLOCK = 4
PAGE_ROW_LIMIT = 256
REC_DEV = 80
N_HOLD = 4


def draw_span_holder(key, part):
    key = jax.random.fold_in(key, 11)
    keys = jax.random.split(key, N_HOLD)
    span_permutations = jax.vmap(lambda single: jax.random.permutation(single, N_HOLD))(keys)
    return span_permutations[:, :SPANS_PER_BLOCK].astype(jnp.int32)


def draw_rec_pos(key, part):
    key = jax.random.fold_in(key, 23)
    keys = jax.random.split(key, LAYERS * N_HOLD)

    def choose(single):
        selected_rows = jax.random.permutation(single, PROMPT_PER_HOLD - 1)[:REC_DEV - 1].astype(jnp.int32)
        last = jnp.full((1,), PROMPT_PER_HOLD - 1, jnp.int32)
        return jnp.sort(jnp.concatenate([selected_rows, last]))
    span_offsets = jax.vmap(choose)(keys).reshape(LAYERS, N_HOLD, REC_DEV)
    base = (jnp.arange(N_HOLD, dtype=jnp.int32) * PROMPT_PER_HOLD)[None, :, None]
    return (span_offsets + base).reshape(LAYERS, N_HOLD * REC_DEV).astype(jnp.int32)


def level_of(rng, dims, pieces, smallest, top_value):
    def one(position, parts):
        heights = jax.random.uniform(jax.random.fold_in(jax.random.fold_in(rng, 6), position), (parts,), jnp.float32, smallest / len(pieces), top_value / len(pieces))
        return jnp.repeat(jnp.exp(heights), dims[position] // parts).reshape((-1,) + (1,) * (len(dims) - position - 1))

    factor_of = one(*pieces[0])
    for cut in pieces[1:]:
        factor_of = factor_of * one(*cut)
    return factor_of


def profile(amount, total, bound, skew):
    portions = [(1 << 20) // math.isqrt(standing ** skew) + 1 for standing in range(2, amount + 1)]
    rest, given = total - bound - (amount - 1), [1] * (amount - 1)
    while rest > 0:
        movable = [i for i in range(amount - 1) if given[i] < bound]
        pool, budget = sum([portions[i] for i in movable]), rest
        for i in movable:
            extra = min(bound - given[i], max(1, budget * portions[i] // pool), rest)
            given[i] = given[i] + extra
            rest = rest - extra
    return np.array([bound] + given)


def ragged(own_key, count, total, bound, slope):
    if count == 2:
        one = jax.random.randint(own_key, (), max(1, total - bound), min(bound, total - 1) + 1)
        return jnp.stack([one, total - one])
    sizes = jnp.asarray(profile(count, total, bound, slope), jnp.int32)
    twos = (count - 1) // 2
    donor, taker = sizes[1:1 + 2 * twos:2], sizes[2:2 + 2 * twos:2]
    margin = jnp.minimum(donor - 1, bound - taker)
    moved = jax.random.randint(jax.random.fold_in(own_key, 1), (twos,), 0, 1 << 20) % (margin + 1)
    sizes = sizes.at[1:1 + 2 * twos:2].set(donor - moved).at[2:2 + 2 * twos:2].set(taker + moved)
    return sizes[jax.random.permutation(jax.random.fold_in(own_key, 2), count)]


def scatter_about(stream_key, shape, spread, bound, cuts=(), kind=jnp.bfloat16):
    loudness = level_of(stream_key, shape, cuts, -0.22, 0.18) if cuts else 1.0
    entries = jax.random.normal(stream_key, shape, jnp.float32) * spread * loudness
    return jnp.minimum(jnp.maximum(entries, -bound), bound).astype(kind)


def setup_inputs(seed: int = 0, part: int = 0) -> dict:
    streams_of = jax.random.split(jax.random.key(seed), 8)
    own_keys = jax.random.split(jax.random.fold_in(streams_of[7], part), 8)
    return {
        "cache_store": scatter_about(own_keys[0], (LAYERS, N_HOLD * N_HOLD, PAGE_ROW_LIMIT, KVH, 2, HD), 1.0, 6.0, ((1, 4), (3, 4))),
        "span_lengths": jax.vmap(lambda own: ragged(own, SPANS_PER_BLOCK, PROMPT_PER_HOLD, PAGE_ROW_LIMIT, 2))(jax.random.split(own_keys[1], N_HOLD)).reshape((N_HOLD, SPANS_PER_BLOCK)).astype(jnp.int32),
        "span_holder": draw_span_holder(jax.random.fold_in(jax.random.fold_in(streams_of[7], part), 71), part),
        "rec_pos": draw_rec_pos(jax.random.fold_in(jax.random.fold_in(streams_of[7], part), 71), part),
        "hidden": scatter_about(own_keys[4], (LAYERS, N_HOLD * REC_DEV, D), 1.0, 6.0, ((1, 4),)),
        "norm_gain": jnp.clip(1.0 + 0.18 * jax.random.normal(streams_of[5], (LAYERS, D), jnp.float32), 0.099609375, 1.8984375).astype(jnp.bfloat16),
        "kv_weight": scatter_about(streams_of[6], (LAYERS, D, KVH, 2, HD), D ** -0.5, 0.0546875, ((1, 4), (2, 4))),
    }


def block_arrangement(lengths, holders_row):
    starts = jnp.cumsum(lengths, axis=1) - lengths
    span_offsets = jnp.arange(PROMPT_PER_HOLD, dtype=jnp.int32)
    which = lax.optimization_barrier(jnp.sum((span_offsets[None, :, None] >= starts[:, None, :]).astype(jnp.int32), axis=2)) - 1
    which = which.astype(jnp.int32)
    holder = jnp.take_along_axis(holders_row, which, axis=1)
    within = span_offsets[None, :] - jnp.take_along_axis(starts, which, axis=1)
    return (holder.astype(jnp.int32), within.astype(jnp.int32))

def reference(cache_store, span_lengths, span_holder, rec_pos, hidden, norm_gain, kv_weight):
    holder, within = block_arrangement(span_lengths, span_holder)
    blocks = jnp.arange(N_HOLD, dtype=jnp.int32)[:, None]
    page_index = (holder * N_HOLD + blocks).reshape(-1)
    page_row = within.reshape(-1)
    united_list = []
    score_list = []
    for layer in range(LAYERS):
        cached = cache_store[layer][page_index, page_row]
        rows_in = hidden[layer].astype(jnp.float32)
        scale = lax.rsqrt(lax.optimization_barrier(jnp.mean(rows_in * rows_in, axis=1, keepdims=True)) + 1e-05)
        normed = (rows_in * scale * norm_gain[layer].astype(jnp.float32)).astype(jnp.bfloat16)
        weight_flat = kv_weight[layer].reshape(D, KVH * 2 * HD)
        fresh = jnp.dot(normed, weight_flat, preferred_element_type=jnp.float32).astype(jnp.bfloat16)
        fresh = fresh.reshape(normed.shape[0], KVH, 2, HD)
        old = cached[rec_pos[layer]].astype(jnp.float32)
        diff = fresh.astype(jnp.float32) - old
        numer = lax.optimization_barrier(jnp.mean(diff * diff, axis=(1, 2, 3)))
        denom = lax.optimization_barrier(jnp.mean(old * old, axis=(1, 2, 3))) + 1e-06
        score_list.append(numer / denom)
        united_list.append(cached.at[rec_pos[layer]].set(fresh))
    return (jnp.stack(united_list), jnp.stack(score_list))
```

```python
import jax
import jax.numpy as jnp
from jax import lax
from jax.sharding import PartitionSpec as P

KVH = 8
PROMPT_PER_HOLD = 512
LAYERS = 2


def block_arrangement(lengths, holders_row):
    starts = jnp.cumsum(lengths, axis=1) - lengths
    span_offsets = jnp.arange(PROMPT_PER_HOLD, dtype=jnp.int32)
    which = (
        jnp.sum((span_offsets[None, :, None] >= starts[:, None, :]).astype(jnp.int32), axis=2) - 1
    )
    holder = jnp.take_along_axis(holders_row, which, axis=1)
    within = span_offsets[None, :] - jnp.take_along_axis(starts, which, axis=1)
    return (holder, within)


def norm_rows(rows, gain):
    rows = rows.astype(jnp.float32)
    scale = lax.rsqrt(jnp.mean(rows * rows, axis=1, keepdims=True) + 1e-05)
    return (rows * scale * gain.astype(jnp.float32)).astype(jnp.bfloat16)


def make_local(n, tps):
    def shift(value, k):
        return lax.ppermute(value, "hold", [(i, (i + k) % n) for i in range(n)])

    def local(cache_store, span_lengths, span_holder, rec_pos, hidden, norm_gain, kv_weight):
        me = lax.axis_index("hold")
        my_tp = lax.axis_index("tp")
        rec = hidden.shape[1]
        width = hidden.shape[2]
        feats = kv_weight.shape[1]
        heads_here, head_size = kv_weight.shape[2], kv_weight.shape[4]
        cols = heads_here * 2 * head_size
        rows_all = LAYERS * rec
        quarter = rows_all // tps

        flat = hidden.reshape(rows_all, width)
        gain_rows = jnp.repeat(norm_gain, rec, axis=0)
        mine = lax.dynamic_slice_in_dim(flat, my_tp * quarter, quarter, axis=0)
        mine_gain = norm_gain[(my_tp * quarter + jnp.arange(quarter)) // rec]
        normed = norm_rows(mine, mine_gain)
        arrived = []
        for k in range(1, n):
            piece = lax.dynamic_slice_in_dim(normed, ((me + k) % n) * feats, feats, axis=1)
            arrived.append(shift(piece, k))

        pages = [lax.dynamic_index_in_dim(cache_store, me, axis=1, keepdims=False)]
        for k in range(1, n):
            page = lax.dynamic_index_in_dim(cache_store, (me + k) % n, axis=1, keepdims=False)
            pages.append(shift(page, k))

        own_full = norm_rows(flat, gain_rows)
        own = lax.dynamic_slice_in_dim(own_full, me * feats, feats, axis=1)
        weight = kv_weight.reshape(LAYERS, feats, cols)
        stacked = jnp.stack(arrived)
        gathered = lax.all_gather(stacked, "tp", axis=1, tiled=True)
        rows = jnp.concatenate([own[None], gathered]).reshape(n, LAYERS, rec, feats)
        partial = jnp.einsum(
            "klrf,lfc->klrc", rows, weight, preferred_element_type=jnp.float32
        )
        odd = partial[1::2]
        odd = jnp.where(me % 2 == 0, jnp.roll(odd, 1, axis=0), odd)
        pairs = [(i, i ^ 1) for i in range(n)]
        summed = partial[0::2] + lax.ppermute(odd, "hold", pairs)
        total = summed[0]
        for k in range(2, n, 2):
            total = total + shift(summed[k // 2], -k)
        fresh = total.astype(jnp.bfloat16).reshape(LAYERS, rec, heads_here, 2, head_size)

        holder, within = block_arrangement(span_lengths, span_holder)
        place = (me - holder[0]) % n
        within = within[0]
        all_pages = jnp.stack(pages, axis=1)
        united_list, squares_list, base_list = [], [], []
        for layer in range(LAYERS):
            cached = all_pages[layer][place, within]
            span_offsets = rec_pos[layer] - me * PROMPT_PER_HOLD
            old = cached[span_offsets].astype(jnp.float32)
            diff = fresh[layer].astype(jnp.float32) - old
            squares_list.append(jnp.sum(diff * diff, axis=(1, 2, 3)))
            base_list.append(jnp.sum(old * old, axis=(1, 2, 3)))
            united_list.append(cached.at[span_offsets].set(fresh[layer]))
        sums = lax.psum(jnp.stack(squares_list + base_list), "tp")
        entries = KVH * 2 * head_size
        deviation = sums[:LAYERS] / entries / (sums[LAYERS:] / entries + 1e-06)
        return (jnp.stack(united_list), deviation)

    return local


def solution(mesh):
    return jax.shard_map(
        make_local(mesh.shape["hold"], mesh.shape["tp"]),
        mesh=mesh,
        in_specs=(
            P(None, ("groups", "hold"), None, "tp", None, None),
            P(("groups", "hold"), None),
            P(("groups", "hold"), None),
            P(None, ("groups", "hold")),
            P(None, ("groups", "hold"), None),
            P(),
            P(None, "hold", "tp", None, None),
        ),
        out_specs=(P(None, ("groups", "hold"), "tp", None, None), P(None, ("groups", "hold"))),
        check_vma=False,
    )
```

```python
import functools

import jax
import jax.numpy as jnp
from jax import lax
from jax.experimental import pallas as pl
from jax.experimental.pallas import tpu as pltpu
from jax.sharding import PartitionSpec as P

KVH = 8
PROMPT_PER_HOLD = 512
LAYERS = 2
CHUNK = 8
VMEM_BYTES = 40 * 1024 * 1024
PARAMS = pltpu.CompilerParams(vmem_limit_bytes=VMEM_BYTES)
ANY = pl.BlockSpec(memory_space=pl.ANY)
VMEM = pl.BlockSpec(memory_space=pltpu.VMEM)
SMEM = pl.BlockSpec(memory_space=pltpu.SMEM)


def norm_rows(rows, gain):
    rows = rows.astype(jnp.float32)
    scale = lax.rsqrt(jnp.mean(rows * rows, axis=1, keepdims=True) + 1e-05)
    return (rows * scale * gain.astype(jnp.float32)).astype(jnp.bfloat16)


def norm_kernel(at, rows_ref, gain_ref, *refs):
    outs, held = refs[:-1], refs[-1]
    quarter, feats = outs[0].shape
    rows = rows_ref[0].astype(jnp.float32)
    mine = rows[:quarter]
    for part in range(1, rows.shape[0] // quarter):
        mine = jnp.where(at[1] == part, rows[part * quarter : (part + 1) * quarter], mine)
    gain = jnp.where(at[0] == 0, gain_ref[0:1], gain_ref[1:2])
    held[...] = norm_rows(mine, gain)
    for k, out in enumerate(outs, 1):
        start = pl.multiple_of(at[1 + k], 128)
        out[...] = held[:, pl.ds(start, feats)]


def normed_share(hidden, gain, me, my_tp, n, tps, feats):
    layers, rec, width = hidden.shape
    quarter = layers * rec // tps
    per_layer = rec // quarter
    at = jnp.stack(
        [my_tp // per_layer, my_tp % per_layer] + [((me + k) % n) * feats for k in range(1, n)]
    ).astype(jnp.int32)
    return pl.pallas_call(
        norm_kernel,
        grid_spec=pltpu.PrefetchScalarGridSpec(
            num_scalar_prefetch=1,
            grid=(1,),
            in_specs=[
                pl.BlockSpec((1, rec, width), lambda i, at: (at[0], 0, 0)),
                pl.BlockSpec(gain.shape, lambda i, at: (0, 0)),
            ],
            out_specs=[pl.BlockSpec((quarter, feats), lambda i, at: (0, 0))] * (n - 1),
            scratch_shapes=[pltpu.VMEM((quarter, width), jnp.bfloat16)],
        ),
        out_shape=[jax.ShapeDtypeStruct((quarter, feats), jnp.bfloat16)] * (n - 1),
        compiler_params=PARAMS,
    )(at, hidden, gain)


def pick_kernel(at, store, *refs):
    out, sem = refs[-2:]
    copy = pltpu.make_async_copy(store.at[:, at[0]], out, sem)
    copy.start()
    copy.wait()


def pick(store, at, after):
    shape = store.shape[:1] + store.shape[2:]
    after = () if after is None else (after,)
    return pl.pallas_call(
        pick_kernel,
        grid_spec=pltpu.PrefetchScalarGridSpec(
            num_scalar_prefetch=1,
            grid=(),
            in_specs=[ANY] * (1 + len(after)),
            out_specs=ANY,
            scratch_shapes=[pltpu.SemaphoreType.DMA],
        ),
        out_shape=jax.ShapeDtypeStruct(shape, store.dtype),
        compiler_params=pltpu.CompilerParams(vmem_limit_bytes=1 << 20),
    )(at.astype(jnp.int32).reshape(1), store, *after)


def unite_kernel(n, starts, lengths, spots, *refs):
    pages, fresh, out, sums, held = refs[:n], refs[n], refs[n + 1], refs[n + 2], refs[n + 3]
    layers, rec = fresh.shape[:2]
    for slot, page in enumerate(pages):
        start, length = starts[slot], lengths[slot]
        whole = length // CHUNK

        def many(i, carry, page=page, start=start):
            for layer in range(layers):
                out[layer, pl.ds(start + i * CHUNK, CHUNK)] = page[layer, pl.ds(i * CHUNK, CHUNK)]
            return carry

        def one(i, carry, page=page, start=start):
            for layer in range(layers):
                out[layer, start + i] = page[layer, i]
            return carry

        lax.fori_loop(0, whole, many, 0)
        lax.fori_loop(whole * CHUNK, length, one, 0)
    for layer in range(layers):

        def renew(j, carry, layer=layer):
            at = layer * rec + j
            spot = spots[at]
            old = out[layer, spot].astype(jnp.float32)
            new = fresh[layer, j]
            diff = new.astype(jnp.float32) - old
            held[pl.ds(at, 1), :] = jnp.sum(jnp.sum(diff * diff, axis=0), axis=0, keepdims=True)
            held[pl.ds(layers * rec + at, 1), :] = jnp.sum(
                jnp.sum(old * old, axis=0), axis=0, keepdims=True
            )
            out[layer, spot] = new
            return carry

        lax.fori_loop(0, rec, renew, 0, unroll=4)
    ones = jnp.ones((8, held.shape[1]), jnp.float32)
    both = lax.dot_general(
        ones,
        held[...],
        (((1,), (1,)), ((), ())),
        precision=lax.Precision.HIGHEST,
        preferred_element_type=jnp.float32,
    )
    sums[...] = both[0:1]


def unite(pages, fresh, starts, lengths, spots):
    n = len(pages)
    layers, rec = fresh.shape[:2]
    row = fresh.shape[2:]
    return pl.pallas_call(
        functools.partial(unite_kernel, n),
        in_specs=[SMEM] * 3 + [VMEM] * (n + 1),
        out_specs=[VMEM, VMEM],
        out_shape=[
            jax.ShapeDtypeStruct((layers, PROMPT_PER_HOLD) + row, fresh.dtype),
            jax.ShapeDtypeStruct((1, 2 * layers * rec), jnp.float32),
        ],
        scratch_shapes=[pltpu.VMEM((2 * layers * rec, row[-1]), jnp.float32)],
        compiler_params=PARAMS,
    )(starts, lengths, spots, *pages, fresh)


def make_local(n, tps):
    def shift(value, k):
        return lax.ppermute(value, "hold", [(i, (i + k) % n) for i in range(n)])

    def swap(value, axis, size, bit):
        return lax.ppermute(value, axis, [(i, i ^ bit) for i in range(size)])

    def local(cache_store, span_lengths, span_holder, rec_pos, hidden, norm_gain, kv_weight):
        me = lax.axis_index("hold")
        my_tp = lax.axis_index("tp")
        rec, width = hidden.shape[1:]
        feats = kv_weight.shape[1]
        heads_here, head_size = kv_weight.shape[2], kv_weight.shape[4]
        cols = heads_here * 2 * head_size
        order = sorted(range(1, n), key=lambda k: (k % 2 == 0, min(k, n - k), k))

        pieces = normed_share(hidden, norm_gain, me, my_tp, n, tps, feats)
        arrived = {k: shift(pieces[k - 1], k) for k in order}

        pages = {0: lax.dynamic_index_in_dim(cache_store, me, axis=1, keepdims=False)}
        sent = []
        for i, k in enumerate(order):
            page = pick(cache_store, (me + k) % n, sent[i - 2] if i >= 2 else None)
            pages[k] = shift(page, k)
            sent.append(pages[k])

        own_full = norm_rows(
            hidden.reshape(LAYERS * rec, width), jnp.repeat(norm_gain, rec, axis=0)
        )
        own = lax.dynamic_slice_in_dim(own_full, me * feats, feats, axis=1)
        weight = kv_weight.reshape(LAYERS, feats, cols)

        def everyone(piece):
            shares = [piece]
            bit = tps // 2
            while bit:
                shares = shares + [swap(share, "tp", tps, bit) for share in shares]
                bit //= 2
            masks = [0]
            bit = tps // 2
            while bit:
                masks = masks + [mask ^ bit for mask in masks]
                bit //= 2
            shares = [shares[masks.index(m)] for m in range(tps)]
            bit = 1
            while bit < tps:
                flip = (my_tp & bit) != 0
                shares = [
                    jnp.where(flip, shares[m ^ bit], shares[m]) for m in range(tps)
                ]
                bit *= 2
            return jnp.concatenate(shares)

        def product(rows):
            return jnp.einsum(
                "lrf,lfc->lrc",
                rows.reshape(LAYERS, rec, feats),
                weight,
                preferred_element_type=jnp.float32,
            )

        partial = {k: product(everyone(arrived[k])) for k in order}
        partial[0] = product(own)
        even = me % 2 == 0
        total = None
        for k in list(range(2, n, 2)) + [0]:
            away = jnp.where(even, partial[(k - 1) % n], partial[(k + 1) % n])
            pair = partial[k] + swap(away, "hold", n, 1)
            pair = shift(pair, -k) if k else pair
            total = pair if total is None else total + pair
        fresh = total.astype(jnp.bfloat16).reshape(LAYERS, rec, heads_here, 2, head_size)

        lengths = span_lengths[0]
        starts = jnp.cumsum(lengths) - lengths
        holders = (me - jnp.arange(n, dtype=jnp.int32)) % n
        held_here = span_holder[0][None, :] == holders[:, None]
        slot_starts = jnp.sum(jnp.where(held_here, starts[None, :], 0), axis=1)
        slot_lengths = jnp.sum(jnp.where(held_here, lengths[None, :], 0), axis=1)
        spots = (rec_pos - me * PROMPT_PER_HOLD).reshape(-1)
        united, sums = unite(
            [pages[k] for k in range(n)], fresh, slot_starts, slot_lengths, spots
        )
        sums = lax.psum(sums, "tp").reshape(2, LAYERS, rec)
        entries = KVH * 2 * head_size
        deviation = sums[0] / entries / (sums[1] / entries + 1e-06)
        return (united, deviation)

    return local


def solution(mesh):
    return jax.shard_map(
        make_local(mesh.shape["hold"], mesh.shape["tp"]),
        mesh=mesh,
        in_specs=(
            P(None, ("groups", "hold"), None, "tp", None, None),
            P(("groups", "hold"), None),
            P(("groups", "hold"), None),
            P(None, ("groups", "hold")),
            P(None, ("groups", "hold"), None),
            P(),
            P(None, "hold", "tp", None, None),
        ),
        out_specs=(P(None, ("groups", "hold"), "tp", None, None), P(None, ("groups", "hold"))),
        check_vma=False,
    )
```

```python
import functools

import jax
import jax.numpy as jnp
from jax import lax
from jax.experimental import pallas as pl
from jax.experimental.pallas import tpu as pltpu
from jax.sharding import PartitionSpec as P

KVH = 8
PROMPT_PER_HOLD = 512
LAYERS = 2
CHUNK = 8
ROWS = 16
VMEM_BYTES = 40 * 1024 * 1024
PARAMS = pltpu.CompilerParams(vmem_limit_bytes=VMEM_BYTES)
HBM = pl.BlockSpec(memory_space=pltpu.HBM)
VMEM = pl.BlockSpec(memory_space=pltpu.VMEM)
SMEM = pl.BlockSpec(memory_space=pltpu.SMEM)


def norm_kernel(at, rows_ref, gain_ref, *refs):
    own, outs, held = refs[0], refs[1:-1], refs[-1]
    rows = rows_ref[...].astype(jnp.float32)
    held[...] = lax.rsqrt(jnp.mean(rows * rows, axis=1, keepdims=True) + 1e-05)
    layer = pl.program_id(0) // (pl.num_programs(0) // gain_ref.shape[0])
    for i, out in enumerate((own,) + outs):
        columns = pl.ds(pl.multiple_of(at[i], 128), out.shape[1])
        gain = gain_ref[0:1, columns].astype(jnp.float32)
        for other in range(1, gain_ref.shape[0]):
            gain = jnp.where(
                layer == other, gain_ref[other : other + 1, columns].astype(jnp.float32), gain
            )
        part = rows_ref[:, columns].astype(jnp.float32)
        out[...] = (part * held[...] * gain).astype(jnp.bfloat16)


def normed_shares(hidden, gain, me, share, n, feats, part):
    layers, rec, width = hidden.shape
    rows = layers * rec
    at = jnp.stack([me * feats] + [((me + k) % n) * feats + share * part for k in range(1, n)])
    sizes = [feats] + [part] * (n - 1)
    return pl.pallas_call(
        norm_kernel,
        grid_spec=pltpu.PrefetchScalarGridSpec(
            num_scalar_prefetch=1,
            grid=(rows // ROWS,),
            in_specs=[
                pl.BlockSpec((ROWS, width), lambda i, at: (i, 0)),
                pl.BlockSpec(gain.shape, lambda i, at: (0, 0)),
            ],
            out_specs=[pl.BlockSpec((ROWS, size), lambda i, at: (i, 0)) for size in sizes],
            scratch_shapes=[pltpu.VMEM((ROWS, 1), jnp.float32)],
        ),
        out_shape=[jax.ShapeDtypeStruct((rows, size), jnp.bfloat16) for size in sizes],
        compiler_params=PARAMS,
    )(at.astype(jnp.int32), hidden.reshape(rows, width), gain)


def pick_kernel(at, store, *refs):
    outs, sems = refs[:-1], refs[-1]
    copies = [
        pltpu.make_async_copy(store.at[:, at[i]], out, sems.at[i]) for i, out in enumerate(outs)
    ]
    for copy in copies:
        copy.start()
    for copy in copies:
        copy.wait()


def pick(store, at):
    shape = store.shape[:1] + store.shape[2:]
    return pl.pallas_call(
        pick_kernel,
        grid_spec=pltpu.PrefetchScalarGridSpec(
            num_scalar_prefetch=1,
            grid=(),
            in_specs=[HBM],
            out_specs=[HBM] * len(at),
            scratch_shapes=[pltpu.SemaphoreType.DMA((len(at),))],
        ),
        out_shape=[jax.ShapeDtypeStruct(shape, store.dtype)] * len(at),
        compiler_params=PARAMS,
    )(jnp.stack(at).astype(jnp.int32), store)


def product_kernel(counts, at, *refs):
    shares, refs = refs[: sum(counts)], refs[sum(counts) :]
    weight, refs = refs[0], refs[1:]
    held, outs = refs[-1], refs[-1 - len(counts) : -1]
    layers, rec, _ = outs[0].shape
    base = 0
    for i, count in enumerate(counts):
        row = pl.multiple_of(at[i] * rec, 16)
        for j in range(count):
            piece = shares[base + j]
            column = pl.multiple_of(at[len(counts) + base + j], 128)
            for layer in range(layers):
                held[layer, pl.ds(row, rec), pl.ds(column, piece.shape[1])] = piece[
                    layer * rec : (layer + 1) * rec
                ]
        base += count
    for layer in range(layers):
        result = jnp.dot(held[layer], weight[layer], preferred_element_type=jnp.float32)
        for i, out in enumerate(outs):
            out[layer] = result[i * rec : (i + 1) * rec]


def products(blocks, weight, order, columns, rec, after):
    counts = tuple(len(block) for block in blocks)
    at = jnp.stack(list(order) + [c for cs in columns for c in cs]).astype(jnp.int32)
    layers, feats, cols = weight.shape
    flat = [share for block in blocks for share in block]
    return pl.pallas_call(
        functools.partial(product_kernel, counts),
        in_specs=[SMEM] + [VMEM] * (len(flat) + 1) + [HBM] * len(after),
        out_specs=[VMEM] * len(blocks),
        out_shape=[jax.ShapeDtypeStruct((layers, rec, cols), jnp.float32)] * len(blocks),
        scratch_shapes=[pltpu.VMEM((layers, len(blocks) * rec, feats), jnp.bfloat16)],
        compiler_params=PARAMS,
    )(at, *flat, weight, *after)


def add_kernel(count, *refs):
    outs = refs[len(refs) - count :]
    for left, right, out in zip(refs[:count], refs[count : 2 * count], outs):
        out[...] = left[...] + right[...]


def add_pairs(left, right, after):
    count = len(left)
    return pl.pallas_call(
        functools.partial(add_kernel, count),
        in_specs=[VMEM] * (2 * count) + [HBM] * len(after),
        out_specs=[VMEM] * count,
        out_shape=[jax.ShapeDtypeStruct(value.shape, value.dtype) for value in left],
        compiler_params=PARAMS,
    )(*left, *right, *after)


def unite_kernel(n, starts, lengths, spots, *refs):
    pages, fresh, out, sums, held = refs[:n], refs[n], refs[n + 1], refs[n + 2], refs[n + 3]
    layers, rec = fresh.shape[:2]
    for slot, page in enumerate(pages):
        start, length = starts[slot], lengths[slot]
        whole = length // CHUNK

        def many(i, carry, page=page, start=start):
            for layer in range(layers):
                out[layer, pl.ds(start + i * CHUNK, CHUNK)] = page[layer, pl.ds(i * CHUNK, CHUNK)]
            return carry

        def one(i, carry, page=page, start=start):
            for layer in range(layers):
                out[layer, start + i] = page[layer, i]
            return carry

        lax.fori_loop(0, whole, many, 0)
        lax.fori_loop(whole * CHUNK, length, one, 0)
    for layer in range(layers):

        def renew(j, carry, layer=layer):
            at = layer * rec + j
            spot = spots[at]
            old = out[layer, spot].astype(jnp.float32)
            new = fresh[layer, j]
            diff = new.astype(jnp.float32) - old
            held[pl.ds(at, 1), :] = jnp.sum(jnp.sum(diff * diff, axis=0), axis=0, keepdims=True)
            held[pl.ds(layers * rec + at, 1), :] = jnp.sum(
                jnp.sum(old * old, axis=0), axis=0, keepdims=True
            )
            out[layer, spot] = new
            return carry

        lax.fori_loop(0, rec, renew, 0, unroll=4)
    ones = jnp.ones((8, held.shape[1]), jnp.float32)
    both = lax.dot_general(
        ones,
        held[...],
        (((1,), (1,)), ((), ())),
        precision=lax.Precision.HIGHEST,
        preferred_element_type=jnp.float32,
    )
    sums[...] = both[0:1]


def unite(pages, fresh, starts, lengths, spots):
    n = len(pages)
    layers, rec = fresh.shape[:2]
    row = fresh.shape[2:]
    return pl.pallas_call(
        functools.partial(unite_kernel, n),
        in_specs=[SMEM] * 3 + [VMEM] * (n + 1),
        out_specs=[VMEM, VMEM],
        out_shape=[
            jax.ShapeDtypeStruct((layers, PROMPT_PER_HOLD) + row, fresh.dtype),
            jax.ShapeDtypeStruct((1, 2 * layers * rec), jnp.float32),
        ],
        scratch_shapes=[pltpu.VMEM((2 * layers * rec, row[-1]), jnp.float32)],
        compiler_params=PARAMS,
    )(starts, lengths, spots, *pages, fresh)


def make_local(n, tps):
    def shift(value, k):
        return lax.ppermute(value, "hold", [(i, (i + k) % n) for i in range(n)])

    def swap(value, axis, size, bit):
        return lax.ppermute(value, axis, [(i, i ^ bit) for i in range(size)])

    def local(cache_store, span_lengths, span_holder, rec_pos, hidden, norm_gain, kv_weight):
        me = lax.axis_index("hold")
        my_tp = lax.axis_index("tp")
        rec = hidden.shape[1]
        feats = kv_weight.shape[1]
        heads_here, head_size = kv_weight.shape[2], kv_weight.shape[4]
        cols = heads_here * 2 * head_size
        odds = sorted(range(1, n, 2), key=lambda k: min(k, n - k))
        evens = sorted(range(2, n, 2), key=lambda k: min(k, n - k))
        cuts = tps
        while feats % (cuts * 128):
            cuts //= 2
        part = feats // cuts
        share = my_tp % cuts

        own, *pieces = normed_shares(hidden, norm_gain, me, share, n, feats, part)
        arrived = {k: shift(pieces[k - 1], k) for k in odds + evens}

        sent = pick(cache_store, [(me + k) % n for k in range(1, n)])
        pages = {k: shift(sent[k - 1], k) for k in odds + evens}
        pages[0] = lax.dynamic_index_in_dim(cache_store, me, axis=1, keepdims=False)

        weight = kv_weight.reshape(LAYERS, feats, cols)

        def everyone(piece):
            shares, masks, bit = [piece], [0], cuts // 2
            while bit:
                shares = shares + [swap(value, "tp", tps, bit) for value in shares]
                masks = masks + [mask ^ bit for mask in masks]
                bit //= 2
            return shares, [(share ^ mask) * part for mask in masks]

        even = me % 2 == 0
        away = [everyone(arrived[k]) for k in odds]
        spot = [jnp.where(even, (k + 1) // 2 % (n // 2), (k - 1) // 2) for k in odds]
        away = products(
            [a[0] for a in away], weight, spot, [a[1] for a in away], rec, [pages[k] for k in odds]
        )
        theirs = [swap(away[i % (n // 2)], "hold", n, 1) for i in range(1, n // 2 + 1)]
        mine = [everyone(arrived[k]) for k in range(2, n, 2)] + [([own], [jnp.int32(0)])]
        mine = products(
            [a[0] for a in mine],
            weight,
            [jnp.int32(i) for i in range(n // 2)],
            [a[1] for a in mine],
            rec,
            [],
        )
        total = mine[-1] + theirs[-1]
        if n > 2:
            pairs = add_pairs(mine[:-1], theirs[:-1], [pages[k] for k in evens])
            for k, pair in zip(range(2, n, 2), pairs):
                total = total + shift(pair, -k)
        fresh = total.astype(jnp.bfloat16).reshape(LAYERS, rec, heads_here, 2, head_size)

        lengths = span_lengths[0]
        starts = jnp.cumsum(lengths) - lengths
        holders = (me - jnp.arange(n, dtype=jnp.int32)) % n
        held_here = span_holder[0][None, :] == holders[:, None]
        slot_starts = jnp.sum(jnp.where(held_here, starts[None, :], 0), axis=1)
        slot_lengths = jnp.sum(jnp.where(held_here, lengths[None, :], 0), axis=1)
        spots = (rec_pos - me * PROMPT_PER_HOLD).reshape(-1)
        united, sums = unite(
            [pages[k] for k in range(n)], fresh, slot_starts, slot_lengths, spots
        )
        sums = lax.psum(sums, "tp").reshape(2, LAYERS, rec)
        entries = KVH * 2 * head_size
        deviation = sums[0] / entries / (sums[1] / entries + 1e-06)
        return (united, deviation)

    return local


def solution(mesh):
    return jax.shard_map(
        make_local(mesh.shape["hold"], mesh.shape["tp"]),
        mesh=mesh,
        in_specs=(
            P(None, ("groups", "hold"), None, "tp", None, None),
            P(("groups", "hold"), None),
            P(("groups", "hold"), None),
            P(None, ("groups", "hold")),
            P(None, ("groups", "hold"), None),
            P(),
            P(None, "hold", "tp", None, None),
        ),
        out_specs=(P(None, ("groups", "hold"), "tp", None, None), P(None, ("groups", "hold"))),
        check_vma=False,
    )
```

```python
import functools

import jax
import jax.numpy as jnp
from jax import lax
from jax.experimental import pallas as pl
from jax.experimental.pallas import tpu as pltpu
from jax.sharding import PartitionSpec as P

KVH = 8
PROMPT_PER_HOLD = 512
LAYERS = 2
CHUNK = 8
ROWS = 16
VMEM_BYTES = 40 * 1024 * 1024
PARAMS = pltpu.CompilerParams(vmem_limit_bytes=VMEM_BYTES)
HBM = pl.BlockSpec(memory_space=pltpu.HBM)
VMEM = pl.BlockSpec(memory_space=pltpu.VMEM)
SMEM = pl.BlockSpec(memory_space=pltpu.SMEM)


def norm_kernel(at, rows_ref, gain_ref, *refs):
    outs, (held, sems) = refs[:-2], refs[-2:]
    step, rec = pl.program_id(0), outs[0].shape[0]
    total = rows_ref.shape[0]

    def fetch(i):
        rows = pl.ds(i * ROWS, ROWS)
        return pltpu.make_async_copy(rows_ref.at[rows], held.at[rows], sems.at[i])

    @pl.when(step == 0)
    def _():
        for i in range(total // ROWS):
            fetch(i).start()

    def gain_of(columns):
        gain = gain_ref[0:1, columns].astype(jnp.float32)
        for other in range(1, gain_ref.shape[0]):
            gain = jnp.where(
                step == other, gain_ref[other : other + 1, columns].astype(jnp.float32), gain
            )
        return gain

    columns = [pl.ds(pl.multiple_of(at[i], 128), out.shape[1]) for i, out in enumerate(outs)]
    for i in range(rec // ROWS):
        fetch(step * (rec // ROWS) + i).wait()
        here = pl.ds(pl.multiple_of(step * rec + i * ROWS, ROWS), ROWS)
        rows = held[here].astype(jnp.float32)
        scale = lax.rsqrt(jnp.mean(rows * rows, axis=1, keepdims=True) + 1e-05)
        for out, column in zip(outs, columns):
            part = held[here, column].astype(jnp.float32)
            out[i * ROWS : (i + 1) * ROWS] = (part * scale * gain_of(column)).astype(jnp.bfloat16)


def normed_shares(hidden, gain, me, share, n, feats, part):
    layers, rec, width = hidden.shape
    rows = layers * rec
    at = jnp.stack([me * feats] + [((me + k) % n) * feats + share * part for k in range(1, n)])
    sizes = [feats] + [part] * (n - 1)
    return pl.pallas_call(
        norm_kernel,
        grid_spec=pltpu.PrefetchScalarGridSpec(
            num_scalar_prefetch=1,
            grid=(layers,),
            in_specs=[HBM, pl.BlockSpec(gain.shape, lambda i, at: (0, 0))],
            out_specs=[pl.BlockSpec((rec, size), lambda i, at: (i, 0)) for size in sizes],
            scratch_shapes=[
                pltpu.VMEM((rows, width), jnp.bfloat16),
                pltpu.SemaphoreType.DMA((rows // ROWS,)),
            ],
        ),
        out_shape=[jax.ShapeDtypeStruct((rows, size), jnp.bfloat16) for size in sizes],
        compiler_params=PARAMS,
    )(at.astype(jnp.int32), hidden.reshape(rows, width), gain)


def tie_kernel(*refs):
    pass


def tie(value, *after):
    return pl.pallas_call(
        tie_kernel,
        in_specs=[HBM] * (1 + len(after)),
        out_specs=HBM,
        out_shape=jax.ShapeDtypeStruct(value.shape, value.dtype),
        input_output_aliases={0: 0},
        compiler_params=PARAMS,
    )(value, *after)


def pick_kernel(wanted, at, store, *refs):
    outs, sems = refs[:-1], refs[-1]
    copies = []
    for i, (out, (k, layer)) in enumerate(zip(outs, wanted)):
        layers = pl.ds(0, out.shape[0]) if layer is None else pl.ds(layer, 1)
        copies.append(pltpu.make_async_copy(store.at[layers, at[k]], out, sems.at[i]))
    for copy in copies:
        copy.start()
    for copy in copies:
        copy.wait()


def pick(store, at, wanted):
    shapes = [
        (store.shape[0] if layer is None else 1,) + store.shape[2:] for _, layer in wanted
    ]
    return pl.pallas_call(
        functools.partial(pick_kernel, wanted),
        grid_spec=pltpu.PrefetchScalarGridSpec(
            num_scalar_prefetch=1,
            grid=(),
            in_specs=[HBM],
            out_specs=[HBM] * len(wanted),
            scratch_shapes=[pltpu.SemaphoreType.DMA((len(wanted),))],
        ),
        out_shape=[jax.ShapeDtypeStruct(shape, store.dtype) for shape in shapes],
        compiler_params=PARAMS,
    )(jnp.stack(at).astype(jnp.int32), store)


def product_kernel(counts, at, *refs):
    shares, weight = refs[: sum(counts)], refs[sum(counts)]
    held, loaded, sems = refs[-3:]
    outs = refs[-3 - len(counts) : -3]
    layers, rec, _ = outs[0].shape
    weights = [
        pltpu.make_async_copy(weight.at[layer], loaded.at[layer], sems.at[0, layer])
        for layer in range(layers)
    ]
    placed = [[] for _ in range(layers)]
    blocks = [i for i, count in enumerate(counts) for _ in range(count)]
    for layer in range(layers):
        for j, (share, i) in enumerate(zip(shares, blocks)):
            row = pl.ds(pl.multiple_of(at[i] * rec, 16), rec)
            column = pl.ds(pl.multiple_of(at[len(counts) + j], 128), share.shape[1])
            placed[layer].append(
                pltpu.make_async_copy(
                    share.at[layer * rec : (layer + 1) * rec],
                    held.at[layer, row, column],
                    sems.at[1 + j, layer],
                )
            )
        for copy in placed[layer] + [weights[layer]]:
            copy.start()
    for layer in range(layers):
        for copy in placed[layer] + [weights[layer]]:
            copy.wait()
        result = jnp.dot(held[layer], loaded[layer], preferred_element_type=jnp.float32)
        for i, out in enumerate(outs):
            out[layer] = result[i * rec : (i + 1) * rec]


def products(blocks, weight, order, columns, rec, after):
    counts = tuple(len(block) for block in blocks)
    at = jnp.stack(list(order) + [c for cs in columns for c in cs]).astype(jnp.int32)
    layers, feats, cols = weight.shape
    flat = [share for block in blocks for share in block]
    return pl.pallas_call(
        functools.partial(product_kernel, counts),
        in_specs=[SMEM] + [HBM] * (len(flat) + 1 + len(after)),
        out_specs=[VMEM] * len(blocks),
        out_shape=[jax.ShapeDtypeStruct((layers, rec, cols), jnp.float32)] * len(blocks),
        scratch_shapes=[
            pltpu.VMEM((layers, len(blocks) * rec, feats), jnp.bfloat16),
            pltpu.VMEM((layers, feats, cols), jnp.bfloat16),
            pltpu.SemaphoreType.DMA((1 + len(flat), layers)),
        ],
        compiler_params=PARAMS,
    )(at, *flat, weight, *after)


def add_kernel(count, *refs):
    outs = refs[len(refs) - count :]
    for left, right, out in zip(refs[:count], refs[count : 2 * count], outs):
        out[...] = left[...] + right[...]


def add_pairs(left, right, after):
    count = len(left)
    return pl.pallas_call(
        functools.partial(add_kernel, count),
        in_specs=[VMEM] * (2 * count) + [HBM] * len(after),
        out_specs=[VMEM] * count,
        out_shape=[jax.ShapeDtypeStruct(value.shape, value.dtype) for value in left],
        compiler_params=PARAMS,
    )(*left, *right, *after)


def unite_kernel(counts, starts, lengths, spots, *refs):
    total = sum(counts)
    fresh, out, sums, held = refs[total:]
    layers, rec = fresh.shape[:2]
    base = 0
    for slot, count in enumerate(counts):
        pages = refs[base : base + count]
        base += count
        start, length = starts[slot], lengths[slot]
        whole = length // CHUNK

        def rows_of(layer, pages=pages):
            return pages[0].at[layer] if len(pages) == 1 else pages[layer].at[0]

        def many(i, carry, rows_of=rows_of, start=start):
            for layer in range(layers):
                out[layer, pl.ds(start + i * CHUNK, CHUNK)] = rows_of(layer)[pl.ds(i * CHUNK, CHUNK)]
            return carry

        def one(i, carry, rows_of=rows_of, start=start):
            for layer in range(layers):
                out[layer, start + i] = rows_of(layer)[i]
            return carry

        lax.fori_loop(0, whole, many, 0)
        lax.fori_loop(whole * CHUNK, length, one, 0)
    for layer in range(layers):

        def renew(j, carry, layer=layer):
            at = layer * rec + j
            spot = spots[at]
            old = out[layer, spot].astype(jnp.float32)
            new = fresh[layer, j]
            diff = new.astype(jnp.float32) - old
            held[pl.ds(at, 1), :] = jnp.sum(jnp.sum(diff * diff, axis=0), axis=0, keepdims=True)
            held[pl.ds(layers * rec + at, 1), :] = jnp.sum(
                jnp.sum(old * old, axis=0), axis=0, keepdims=True
            )
            out[layer, spot] = new
            return carry

        lax.fori_loop(0, rec, renew, 0, unroll=4)
    ones = jnp.ones((8, held.shape[1]), jnp.float32)
    both = lax.dot_general(
        ones,
        held[...],
        (((1,), (1,)), ((), ())),
        precision=lax.Precision.HIGHEST,
        preferred_element_type=jnp.float32,
    )
    sums[...] = both[0:1]


def unite(pages, fresh, starts, lengths, spots):
    counts = tuple(len(page) for page in pages)
    flat = [piece for page in pages for piece in page]
    layers, rec = fresh.shape[:2]
    row = fresh.shape[2:]
    return pl.pallas_call(
        functools.partial(unite_kernel, counts),
        in_specs=[SMEM] * 3 + [VMEM] * (len(flat) + 1),
        out_specs=[VMEM, VMEM],
        out_shape=[
            jax.ShapeDtypeStruct((layers, PROMPT_PER_HOLD) + row, fresh.dtype),
            jax.ShapeDtypeStruct((1, 2 * layers * rec), jnp.float32),
        ],
        scratch_shapes=[pltpu.VMEM((2 * layers * rec, row[-1]), jnp.float32)],
        compiler_params=PARAMS,
    )(starts, lengths, spots, *flat, fresh)


def make_local(n, tps):
    def shift(value, k):
        return lax.ppermute(value, "hold", [(i, (i + k) % n) for i in range(n)])

    def swap(value, axis, size, bit):
        return lax.ppermute(value, axis, [(i, i ^ bit) for i in range(size)])

    def local(cache_store, span_lengths, span_holder, rec_pos, hidden, norm_gain, kv_weight):
        me = lax.axis_index("hold")
        my_tp = lax.axis_index("tp")
        rec = hidden.shape[1]
        feats = kv_weight.shape[1]
        heads_here, head_size = kv_weight.shape[2], kv_weight.shape[4]
        cols = heads_here * 2 * head_size
        odds = sorted(range(1, n, 2), key=lambda k: min(k, n - k))
        evens = sorted(range(2, n, 2), key=lambda k: min(k, n - k))
        cuts = tps
        while feats % (cuts * 128):
            cuts //= 2
        part = feats // cuts
        share = my_tp % cuts

        wanted = [(k, None) for k in odds] + [(k, layer) for k in evens for layer in range(LAYERS)]
        sent = pick(cache_store, [(me + k) % n for k in range(n)], wanted)
        pages = {k: [] for k in range(n)}
        for (k, _), page in zip(wanted, sent):
            pages[k].append(shift(page, k))
        pages[0] = [lax.dynamic_index_in_dim(cache_store, me, axis=1, keepdims=False)]

        own, *pieces = normed_shares(hidden, norm_gain, me, share, n, feats, part)
        arrived = {k: shift(pieces[k - 1], k) for k in odds + evens}
        weight = kv_weight.reshape(LAYERS, feats, cols)
        arrived[odds[0]] = tie(arrived[odds[0]], weight, *pages[odds[0]])
        early = [page for k in odds[1:] for page in pages[k]]
        halves = [[pages[k][layer] for k in evens] for layer in range(LAYERS)]

        def everyone(piece):
            shares, masks, bit = [piece], [0], cuts // 2
            while bit:
                shares = shares + [swap(value, "tp", tps, bit) for value in shares]
                masks = masks + [mask ^ bit for mask in masks]
                bit //= 2
            return shares, [(share ^ mask) * part for mask in masks]

        even = me % 2 == 0
        away = [everyone(arrived[k]) for k in odds]
        spot = [jnp.where(even, (k + 1) // 2 % (n // 2), (k - 1) // 2) for k in odds]
        away = products(
            [a[0] for a in away], weight, spot, [a[1] for a in away], rec, early
        )
        theirs = [swap(away[i % (n // 2)], "hold", n, 1) for i in range(1, n // 2 + 1)]
        mine = [everyone(arrived[k]) for k in range(2, n, 2)] + [([own], [jnp.int32(0)])]
        mine = products(
            [a[0] for a in mine],
            weight,
            [jnp.int32(i) for i in range(n // 2)],
            [a[1] for a in mine],
            rec,
            halves[0],
        )
        total = mine[-1] + theirs[-1]
        if n > 2:
            pairs = add_pairs(mine[:-1], theirs[:-1], halves[1])
            for k, pair in zip(range(2, n, 2), pairs):
                total = total + shift(pair, -k)
        fresh = total.astype(jnp.bfloat16).reshape(LAYERS, rec, heads_here, 2, head_size)

        lengths = span_lengths[0]
        starts = jnp.cumsum(lengths) - lengths
        holders = (me - jnp.arange(n, dtype=jnp.int32)) % n
        held_here = span_holder[0][None, :] == holders[:, None]
        slot_starts = jnp.sum(jnp.where(held_here, starts[None, :], 0), axis=1)
        slot_lengths = jnp.sum(jnp.where(held_here, lengths[None, :], 0), axis=1)
        spots = (rec_pos - me * PROMPT_PER_HOLD).reshape(-1)
        united, sums = unite(
            [pages[k] for k in range(n)], fresh, slot_starts, slot_lengths, spots
        )
        sums = lax.psum(sums, "tp").reshape(2, LAYERS, rec)
        entries = KVH * 2 * head_size
        deviation = sums[0] / entries / (sums[1] / entries + 1e-06)
        return (united, deviation)

    return local


def solution(mesh):
    return jax.shard_map(
        make_local(mesh.shape["hold"], mesh.shape["tp"]),
        mesh=mesh,
        in_specs=(
            P(None, ("groups", "hold"), None, "tp", None, None),
            P(("groups", "hold"), None),
            P(("groups", "hold"), None),
            P(None, ("groups", "hold")),
            P(None, ("groups", "hold"), None),
            P(),
            P(None, "hold", "tp", None, None),
        ),
        out_specs=(P(None, ("groups", "hold"), "tp", None, None), P(None, ("groups", "hold"))),
        check_vma=False,
    )
```

```python
import functools

import jax
import jax.numpy as jnp
from jax import lax
from jax.experimental import pallas as pl
from jax.experimental.pallas import tpu as pltpu
from jax.sharding import PartitionSpec as P

KVH = 8
PROMPT_PER_HOLD = 512
LAYERS = 2
CHUNK = 8
ROWS = 16
UNROLL = 8
CUTS = 3
VMEM_BYTES = 16 * 1024 * 1024
FREE = pl.CostEstimate(flops=0, bytes_accessed=0, transcendentals=0)
PARAMS = pltpu.CompilerParams(vmem_limit_bytes=VMEM_BYTES)
WIDE = pltpu.CompilerParams(vmem_limit_bytes=60 * 1024 * 1024)
ANY = pl.BlockSpec(memory_space=pl.ANY)
VMEM = pl.BlockSpec(memory_space=pltpu.VMEM)
SMEM = pl.BlockSpec(memory_space=pltpu.SMEM)


def norm_kernel(at, rows_ref, gain_ref, *refs):
    own, outs, held = refs[0], refs[1:-1], refs[-1]
    rows = rows_ref[...].astype(jnp.float32)
    held[...] = lax.rsqrt(jnp.mean(rows * rows, axis=1, keepdims=True) + 1e-05)
    layer = pl.program_id(0) // (pl.num_programs(0) // gain_ref.shape[0])
    for i, out in enumerate((own,) + outs):
        columns = pl.ds(pl.multiple_of(at[i], 128), out.shape[1])
        gain = gain_ref[0:1, columns].astype(jnp.float32)
        for other in range(1, gain_ref.shape[0]):
            gain = jnp.where(
                layer == other, gain_ref[other : other + 1, columns].astype(jnp.float32), gain
            )
        part = rows_ref[:, columns].astype(jnp.float32)
        out[...] = (part * held[...] * gain).astype(jnp.bfloat16)


def normed_shares(hidden, gain, me, share, n, feats, part):
    layers, rec, width = hidden.shape
    rows = layers * rec
    at = jnp.stack([me * feats] + [((me + k) % n) * feats + share * part for k in range(1, n)])
    sizes = [feats] + [part] * (n - 1)
    return pl.pallas_call(
        norm_kernel,
        grid_spec=pltpu.PrefetchScalarGridSpec(
            num_scalar_prefetch=1,
            grid=(rows // ROWS,),
            in_specs=[
                pl.BlockSpec((ROWS, width), lambda i, at: (i, 0)),
                pl.BlockSpec(gain.shape, lambda i, at: (0, 0)),
            ],
            out_specs=[pl.BlockSpec((ROWS, size), lambda i, at: (i, 0)) for size in sizes],
            scratch_shapes=[pltpu.VMEM((ROWS, 1), jnp.float32)],
        ),
        out_shape=[jax.ShapeDtypeStruct((rows, size), jnp.bfloat16) for size in sizes],
        cost_estimate=FREE,
        compiler_params=PARAMS,
    )(at.astype(jnp.int32), hidden.reshape(rows, width), gain)


def tie_kernel(*refs):
    pass


def tie(value, *after):
    return pl.pallas_call(
        tie_kernel,
        in_specs=[ANY] * (1 + len(after)),
        out_specs=ANY,
        out_shape=jax.ShapeDtypeStruct(value.shape, value.dtype),
        input_output_aliases={0: 0},
        cost_estimate=FREE,
        compiler_params=PARAMS,
    )(value, *after)


def pick_kernel(wanted, at, store, *refs):
    outs, held, sems = refs[: len(wanted)], refs[-2], refs[-1]
    moves = []
    for i, (out, (k, layer)) in enumerate(zip(outs, wanted)):
        for j in range(out.shape[0]):
            slot = len(moves)
            source = store.at[j if layer is None else layer, at[k]]
            fetch = pltpu.make_async_copy(source, held.at[slot], sems.at[0, slot])
            fetch.start()
            moves.append((fetch, pltpu.make_async_copy(held.at[slot], out.at[j], sems.at[1, slot])))
    for fetch, place in moves:
        fetch.wait()
        place.start()
    for _, place in moves:
        place.wait()


def pick(store, at, wanted):
    if not wanted:
        return []
    counts = [store.shape[0] if layer is None else 1 for _, layer in wanted]
    total = sum(counts)
    return pl.pallas_call(
        functools.partial(pick_kernel, wanted),
        grid_spec=pltpu.PrefetchScalarGridSpec(
            num_scalar_prefetch=1,
            grid=(),
            in_specs=[ANY],
            out_specs=[ANY] * len(wanted),
            scratch_shapes=[
                pltpu.VMEM((total,) + store.shape[2:], store.dtype),
                pltpu.SemaphoreType.DMA((2, total)),
            ],
        ),
        out_shape=[
            jax.ShapeDtypeStruct((count,) + store.shape[2:], store.dtype) for count in counts
        ],
        cost_estimate=FREE,
        compiler_params=WIDE,
    )(jnp.stack(at).astype(jnp.int32), store)


def product_kernel(counts, at, *refs):
    weight, shares = refs[0], refs[1 : 1 + sum(counts)]
    held, loaded, sems, weight_sems = refs[-4:]
    outs = refs[-4 - len(counts) : -4]
    layers, rec, _ = outs[0].shape
    blocks = [i for i, count in enumerate(counts) for _ in range(count)]
    cuts = weight_sems.shape[1]
    chunk = weight.shape[1] // cuts
    placed, weights = [], []
    for layer in range(layers):
        placed.append([])
        for j, (share, i) in enumerate(zip(shares, blocks)):
            row = pl.ds(pl.multiple_of(at[i] * rec, 16), rec)
            column = pl.ds(pl.multiple_of(at[len(counts) + j], 128), share.shape[1])
            source, target = share.at[layer * rec : (layer + 1) * rec], held.at[layer, row, column]
            placed[layer].append(pltpu.make_async_copy(source, target, sems.at[j, layer]))
        weights.append([])
        for c in range(cuts):
            piece = pl.ds(c * chunk, chunk)
            source, target = weight.at[layer, piece], loaded.at[layer, piece]
            weights[layer].append(pltpu.make_async_copy(source, target, weight_sems.at[layer, c]))
        for copy in placed[layer] + weights[layer]:
            copy.start()
    for layer in range(layers):
        for copy in placed[layer]:
            copy.wait()
        total = None
        for c in range(cuts):
            weights[layer][c].wait()
            piece = slice(c * chunk, (c + 1) * chunk)
            result = jnp.dot(
                held[layer, :, piece], loaded[layer, piece], preferred_element_type=jnp.float32
            )
            total = result if total is None else total + result
        for i, out in enumerate(outs):
            out[layer] = total[i * rec : (i + 1) * rec]


def products(blocks, weight, order, columns, rec):
    counts = tuple(len(block) for block in blocks)
    at = jnp.stack(list(order) + [c for cs in columns for c in cs]).astype(jnp.int32)
    layers, feats, cols = weight.shape
    flat = [share for block in blocks for share in block]
    return pl.pallas_call(
        functools.partial(product_kernel, counts),
        in_specs=[SMEM] + [ANY] * (1 + len(flat)),
        out_specs=[VMEM] * len(blocks),
        out_shape=[jax.ShapeDtypeStruct((layers, rec, cols), jnp.float32)] * len(blocks),
        scratch_shapes=[
            pltpu.VMEM((layers, len(blocks) * rec, feats), jnp.bfloat16),
            pltpu.VMEM((layers, feats, cols), jnp.bfloat16),
            pltpu.SemaphoreType.DMA((len(flat), layers)),
            pltpu.SemaphoreType.DMA((layers, CUTS)),
        ],
        cost_estimate=FREE,
        compiler_params=WIDE,
    )(at, weight, *flat)


def add_kernel(count, *refs):
    outs = refs[len(refs) - count :]
    for left, right, out in zip(refs[:count], refs[count : 2 * count], outs):
        out[...] = left[...] + right[...]


def add_pairs(left, right):
    count = len(left)
    return pl.pallas_call(
        functools.partial(add_kernel, count),
        in_specs=[VMEM] * (2 * count),
        out_specs=[VMEM] * count,
        out_shape=[jax.ShapeDtypeStruct(value.shape, value.dtype) for value in left],
        cost_estimate=FREE,
        compiler_params=PARAMS,
    )(*left, *right)


def unite_kernel(counts, starts, lengths, spots, *refs):
    total = sum(counts)
    pages, (fresh, out, sums, held, squares, sems) = refs[:total], refs[total:]
    layers, rec = fresh.shape[:2]
    copies, base = [], 0
    for slot, count in enumerate(counts):
        copies.append([])
        for i in range(count):
            target = held.at[slot] if count == 1 else held.at[slot, pl.ds(i, 1)]
            copies[-1].append(pltpu.make_async_copy(pages[base + i], target, sems.at[base + i]))
            copies[-1][-1].start()
        base += count
    for slot in range(len(counts)):
        for copy in copies[slot]:
            copy.wait()
        start, length = starts[slot], lengths[slot]
        whole = length // CHUNK

        def many(i, carry, slot=slot, start=start):
            for layer in range(layers):
                out[layer, pl.ds(start + i * CHUNK, CHUNK)] = held[
                    slot, layer, pl.ds(i * CHUNK, CHUNK)
                ]
            return carry

        def one(i, carry, slot=slot, start=start):
            for layer in range(layers):
                out[layer, start + i] = held[slot, layer, i]
            return carry

        lax.fori_loop(0, whole, many, 0)
        lax.fori_loop(whole * CHUNK, length, one, 0)
    for layer in range(layers):

        def renew(j, carry, layer=layer):
            at = layer * rec + j
            spot = spots[at]
            old = out[layer, spot].astype(jnp.float32)
            new = fresh[layer, j]
            diff = new.astype(jnp.float32) - old
            squares[pl.ds(at, 1), :] = jnp.sum(jnp.sum(diff * diff, axis=0), axis=0, keepdims=True)
            squares[pl.ds(layers * rec + at, 1), :] = jnp.sum(
                jnp.sum(old * old, axis=0), axis=0, keepdims=True
            )
            out[layer, spot] = new
            return carry

        lax.fori_loop(0, rec, renew, 0, unroll=UNROLL)
    ones = jnp.ones((8, squares.shape[1]), jnp.float32)
    both = lax.dot_general(
        ones,
        squares[...],
        (((1,), (1,)), ((), ())),
        precision=lax.Precision.HIGHEST,
        preferred_element_type=jnp.float32,
    )
    sums[...] = both[0:1]


def unite(pages, fresh, starts, lengths, spots):
    counts = tuple(len(page) for page in pages)
    flat = [piece for page in pages for piece in page]
    layers, rec = fresh.shape[:2]
    rows = flat[0].shape[1:]
    return pl.pallas_call(
        functools.partial(unite_kernel, counts),
        in_specs=[SMEM] * 3 + [ANY] * len(flat) + [VMEM],
        out_specs=[VMEM, VMEM],
        out_shape=[
            jax.ShapeDtypeStruct((layers, PROMPT_PER_HOLD) + rows[1:], fresh.dtype),
            jax.ShapeDtypeStruct((1, 2 * layers * rec), jnp.float32),
        ],
        scratch_shapes=[
            pltpu.VMEM((len(pages), layers) + rows, fresh.dtype),
            pltpu.VMEM((2 * layers * rec, rows[-1]), jnp.float32),
            pltpu.SemaphoreType.DMA((len(flat),)),
        ],
        cost_estimate=FREE,
        compiler_params=PARAMS,
    )(starts, lengths, spots, *flat, fresh)


def make_local(n, tps):
    def shift(value, k):
        return lax.ppermute(value, "hold", [(i, (i + k) % n) for i in range(n)])

    def swap(value, axis, size, bit):
        return lax.ppermute(value, axis, [(i, i ^ bit) for i in range(size)])

    def local(cache_store, span_lengths, span_holder, rec_pos, hidden, norm_gain, kv_weight):
        me = lax.axis_index("hold")
        my_tp = lax.axis_index("tp")
        rec = hidden.shape[1]
        feats = kv_weight.shape[1]
        heads_here, head_size = kv_weight.shape[2], kv_weight.shape[4]
        cols = heads_here * 2 * head_size
        odds = sorted(range(1, n, 2), key=lambda k: min(k, n - k))
        evens = sorted(range(2, n, 2), key=lambda k: min(k, n - k))
        cuts = tps
        while feats % (cuts * 128):
            cuts //= 2
        part = feats // cuts
        share = my_tp % cuts

        own, *pieces = normed_shares(hidden, norm_gain, me, share, n, feats, part)
        arrived = {k: shift(pieces[k - 1], k) for k in odds + evens}
        at = [(me + k) % n for k in range(n)]
        names = [(k, None) for k in odds[::-1]] + [(k, i) for k in evens for i in range(LAYERS)]
        picked = pick(cache_store, at, names + [(0, None)])
        there, last = {}, ()
        for name, page in zip(names, picked):
            there[name] = shift(tie(page, *last) if last else page, name[0])
            last = (there[name],)
        pages = [[picked[-1]]] + [
            [there[name] for name in sorted(names, key=lambda x: x[1] or 0) if name[0] == k]
            for k in range(1, n)
        ]

        weight = kv_weight.reshape(LAYERS, feats, cols)
        arrived[odds[0]] = tie(arrived[odds[0]], weight[:1, :8, :128])

        def everyone(piece):
            shares, masks, bit = [piece], [0], cuts // 2
            while bit:
                shares = shares + [swap(value, "tp", tps, bit) for value in shares]
                masks = masks + [mask ^ bit for mask in masks]
                bit //= 2
            return shares, [(share ^ mask) * part for mask in masks]

        even = me % 2 == 0
        half = n // 2
        blocks = [everyone(arrived[k]) for k in odds + evens] + [([own], [jnp.int32(0)])]
        order = [jnp.where(even, (k + 1) // 2 % half, (k - 1) // 2) for k in odds]
        order += [jnp.int32(half + k // 2) for k in evens + [0]]
        partial = products(
            [a[0] for a in blocks], weight, order, [a[1] for a in blocks], rec
        )
        theirs = [swap(partial[i % half], "hold", n, 1) for i in range(1, half + 1)]
        mine = [*partial[half + 1 :], partial[half]]
        total = mine[-1] + theirs[-1]
        if n > 2:
            pairs = add_pairs(mine[:-1], theirs[:-1])
            for k, pair in zip(range(2, n, 2), pairs):
                total = total + shift(pair, -k)
        fresh = total.astype(jnp.bfloat16).reshape(LAYERS, rec, heads_here, 2, head_size)

        lengths = span_lengths[0]
        starts = jnp.cumsum(lengths) - lengths
        holders = (me - jnp.arange(n, dtype=jnp.int32)) % n
        held_here = span_holder[0][None, :] == holders[:, None]
        slot_starts = jnp.sum(jnp.where(held_here, starts[None, :], 0), axis=1)
        slot_lengths = jnp.sum(jnp.where(held_here, lengths[None, :], 0), axis=1)
        spots = (rec_pos - me * PROMPT_PER_HOLD).reshape(-1)
        united, sums = unite(pages, fresh, slot_starts, slot_lengths, spots)
        sums = lax.psum(sums, "tp").reshape(2, LAYERS, rec)
        entries = KVH * 2 * head_size
        deviation = sums[0] / entries / (sums[1] / entries + 1e-06)
        return (united, deviation)

    return local


def solution(mesh):
    return jax.shard_map(
        make_local(mesh.shape["hold"], mesh.shape["tp"]),
        mesh=mesh,
        in_specs=(
            P(None, ("groups", "hold"), None, "tp", None, None),
            P(("groups", "hold"), None),
            P(("groups", "hold"), None),
            P(None, ("groups", "hold")),
            P(None, ("groups", "hold"), None),
            P(),
            P(None, "hold", "tp", None, None),
        ),
        out_specs=(P(None, ("groups", "hold"), "tp", None, None), P(None, ("groups", "hold"))),
        check_vma=False,
    )
```

```python
import functools

import jax
import jax.numpy as jnp
from jax import lax
from jax.experimental import pallas as pl
from jax.experimental.pallas import tpu as pltpu
from jax.sharding import PartitionSpec as P

KVH = 8
PROMPT_PER_HOLD = 512
LAYERS = 2
CHUNK = 8
ROWS = 16
UNROLL = 8
CUTS = 3
VMEM_BYTES = 16 * 1024 * 1024
FREE = pl.CostEstimate(flops=0, bytes_accessed=0, transcendentals=0)
PARAMS = pltpu.CompilerParams(vmem_limit_bytes=VMEM_BYTES)
WIDE = pltpu.CompilerParams(vmem_limit_bytes=60 * 1024 * 1024)
ANY = pl.BlockSpec(memory_space=pl.ANY)
VMEM = pl.BlockSpec(memory_space=pltpu.VMEM)
SMEM = pl.BlockSpec(memory_space=pltpu.SMEM)


def norm_kernel(at, rows_ref, gain_ref, *outs):
    layers = gain_ref.shape[0]
    rec = rows_ref.shape[0] // layers
    columns = [pl.ds(pl.multiple_of(at[i], 128), out.shape[1]) for i, out in enumerate(outs)]
    for layer in range(layers):
        gains = [gain_ref[layer : layer + 1, column].astype(jnp.float32) for column in columns]

        def chunk(i, carry, layer=layer, gains=gains):
            here = pl.ds(pl.multiple_of(layer * rec + i * ROWS, ROWS), ROWS)
            rows = rows_ref[here, :].astype(jnp.float32)
            scale = lax.rsqrt(jnp.mean(rows * rows, axis=1, keepdims=True) + 1e-05)
            for out, column, gain in zip(outs, columns, gains):
                part = rows_ref[here, column].astype(jnp.float32)
                out[here, :] = (part * scale * gain).astype(jnp.bfloat16)
            return carry

        lax.fori_loop(0, rec // ROWS, chunk, 0)


def normed_shares(hidden, gain, me, share, n, feats, part):
    layers, rec, width = hidden.shape
    rows = layers * rec
    at = jnp.stack([me * feats] + [((me + k) % n) * feats + share * part for k in range(1, n)])
    sizes = [feats] + [part] * (n - 1)
    return pl.pallas_call(
        norm_kernel,
        in_specs=[SMEM, VMEM, VMEM],
        out_specs=[VMEM] * n,
        out_shape=[jax.ShapeDtypeStruct((rows, size), jnp.bfloat16) for size in sizes],
        cost_estimate=FREE,
        compiler_params=PARAMS,
    )(at.astype(jnp.int32), hidden.reshape(rows, width), gain)


def tie_kernel(*refs):
    pass


def tie(value, *after):
    return pl.pallas_call(
        tie_kernel,
        in_specs=[ANY] * (1 + len(after)),
        out_specs=ANY,
        out_shape=jax.ShapeDtypeStruct(value.shape, value.dtype),
        input_output_aliases={0: 0},
        cost_estimate=FREE,
        compiler_params=PARAMS,
    )(value, *after)


def pick_kernel(wanted, at, store, *refs):
    outs, held, sems = refs[: len(wanted)], refs[-2], refs[-1]
    moves = []
    for i, (out, (k, layer)) in enumerate(zip(outs, wanted)):
        for j in range(out.shape[0]):
            slot = len(moves)
            source = store.at[j if layer is None else layer, at[k]]
            fetch = pltpu.make_async_copy(source, held.at[slot], sems.at[0, slot])
            fetch.start()
            moves.append((fetch, pltpu.make_async_copy(held.at[slot], out.at[j], sems.at[1, slot])))
    for fetch, place in moves:
        fetch.wait()
        place.start()
    for _, place in moves:
        place.wait()


def pick(store, at, wanted):
    if not wanted:
        return []
    counts = [store.shape[0] if layer is None else 1 for _, layer in wanted]
    total = sum(counts)
    return pl.pallas_call(
        functools.partial(pick_kernel, wanted),
        grid_spec=pltpu.PrefetchScalarGridSpec(
            num_scalar_prefetch=1,
            grid=(),
            in_specs=[ANY],
            out_specs=[ANY] * len(wanted),
            scratch_shapes=[
                pltpu.VMEM((total,) + store.shape[2:], store.dtype),
                pltpu.SemaphoreType.DMA((2, total)),
            ],
        ),
        out_shape=[
            jax.ShapeDtypeStruct((count,) + store.shape[2:], store.dtype) for count in counts
        ],
        cost_estimate=FREE,
        compiler_params=WIDE,
    )(jnp.stack(at).astype(jnp.int32), store)


def product_kernel(counts, at, *refs):
    weight, shares = refs[0], refs[1 : 1 + sum(counts)]
    held, loaded, sems, weight_sems = refs[-4:]
    outs = refs[-4 - len(counts) : -4]
    layers, rec, _ = outs[0].shape
    blocks = [i for i, count in enumerate(counts) for _ in range(count)]
    cuts = weight_sems.shape[1]
    chunk = weight.shape[1] // cuts
    placed, weights = [], []
    for layer in range(layers):
        placed.append([])
        for j, (share, i) in enumerate(zip(shares, blocks)):
            row = pl.ds(pl.multiple_of(at[i] * rec, 16), rec)
            column = pl.ds(pl.multiple_of(at[len(counts) + j], 128), share.shape[1])
            source, target = share.at[layer * rec : (layer + 1) * rec], held.at[layer, row, column]
            placed[layer].append(pltpu.make_async_copy(source, target, sems.at[j, layer]))
        weights.append([])
        for c in range(cuts):
            piece = pl.ds(c * chunk, chunk)
            source, target = weight.at[layer, piece], loaded.at[layer, piece]
            weights[layer].append(pltpu.make_async_copy(source, target, weight_sems.at[layer, c]))
        for copy in placed[layer] + weights[layer]:
            copy.start()
    for layer in range(layers):
        for copy in placed[layer]:
            copy.wait()
        total = None
        for c in range(cuts):
            weights[layer][c].wait()
            piece = slice(c * chunk, (c + 1) * chunk)
            result = jnp.dot(
                held[layer, :, piece], loaded[layer, piece], preferred_element_type=jnp.float32
            )
            total = result if total is None else total + result
        for i, out in enumerate(outs):
            out[layer] = total[i * rec : (i + 1) * rec]


def products(blocks, weight, order, columns, rec):
    counts = tuple(len(block) for block in blocks)
    at = jnp.stack(list(order) + [c for cs in columns for c in cs]).astype(jnp.int32)
    layers, feats, cols = weight.shape
    flat = [share for block in blocks for share in block]
    return pl.pallas_call(
        functools.partial(product_kernel, counts),
        in_specs=[SMEM] + [ANY] * (1 + len(flat)),
        out_specs=[VMEM] * len(blocks),
        out_shape=[jax.ShapeDtypeStruct((layers, rec, cols), jnp.float32)] * len(blocks),
        scratch_shapes=[
            pltpu.VMEM((layers, len(blocks) * rec, feats), jnp.bfloat16),
            pltpu.VMEM((layers, feats, cols), jnp.bfloat16),
            pltpu.SemaphoreType.DMA((len(flat), layers)),
            pltpu.SemaphoreType.DMA((layers, CUTS)),
        ],
        cost_estimate=FREE,
        compiler_params=WIDE,
    )(at, weight, *flat)


def add_kernel(count, *refs):
    outs = refs[len(refs) - count :]
    for left, right, out in zip(refs[:count], refs[count : 2 * count], outs):
        out[...] = left[...] + right[...]


def add_pairs(left, right):
    count = len(left)
    return pl.pallas_call(
        functools.partial(add_kernel, count),
        in_specs=[VMEM] * (2 * count),
        out_specs=[VMEM] * count,
        out_shape=[jax.ShapeDtypeStruct(value.shape, value.dtype) for value in left],
        cost_estimate=FREE,
        compiler_params=PARAMS,
    )(*left, *right)


def unite_kernel(counts, starts, lengths, spots, *refs):
    total = sum(counts)
    pages, (fresh, out, sums, held, squares, sems) = refs[:total], refs[total:]
    layers, rec = fresh.shape[:2]
    copies, base = [], 0
    for slot, count in enumerate(counts):
        copies.append([])
        for i in range(count):
            target = held.at[slot] if count == 1 else held.at[slot, pl.ds(i, 1)]
            copies[-1].append(pltpu.make_async_copy(pages[base + i], target, sems.at[base + i]))
            copies[-1][-1].start()
        base += count
    for slot in range(len(counts)):
        for copy in copies[slot]:
            copy.wait()
        start, length = starts[slot], lengths[slot]
        whole = length // CHUNK

        def many(i, carry, slot=slot, start=start):
            for layer in range(layers):
                out[layer, pl.ds(start + i * CHUNK, CHUNK)] = held[
                    slot, layer, pl.ds(i * CHUNK, CHUNK)
                ]
            return carry

        def one(i, carry, slot=slot, start=start):
            for layer in range(layers):
                out[layer, start + i] = held[slot, layer, i]
            return carry

        lax.fori_loop(0, whole, many, 0)
        lax.fori_loop(whole * CHUNK, length, one, 0)
    for layer in range(layers):

        def renew(j, carry, layer=layer):
            at = layer * rec + j
            spot = spots[at]
            old = out[layer, spot].astype(jnp.float32)
            new = fresh[layer, j]
            diff = new.astype(jnp.float32) - old
            squares[pl.ds(at, 1), :] = jnp.sum(jnp.sum(diff * diff, axis=0), axis=0, keepdims=True)
            squares[pl.ds(layers * rec + at, 1), :] = jnp.sum(
                jnp.sum(old * old, axis=0), axis=0, keepdims=True
            )
            out[layer, spot] = new
            return carry

        lax.fori_loop(0, rec, renew, 0, unroll=UNROLL)
    ones = jnp.ones((8, squares.shape[1]), jnp.float32)
    both = lax.dot_general(
        ones,
        squares[...],
        (((1,), (1,)), ((), ())),
        precision=lax.Precision.HIGHEST,
        preferred_element_type=jnp.float32,
    )
    sums[...] = both[0:1]


def unite(pages, fresh, starts, lengths, spots):
    counts = tuple(len(page) for page in pages)
    flat = [piece for page in pages for piece in page]
    layers, rec = fresh.shape[:2]
    rows = flat[0].shape[1:]
    return pl.pallas_call(
        functools.partial(unite_kernel, counts),
        in_specs=[SMEM] * 3 + [ANY] * len(flat) + [VMEM],
        out_specs=[VMEM, VMEM],
        out_shape=[
            jax.ShapeDtypeStruct((layers, PROMPT_PER_HOLD) + rows[1:], fresh.dtype),
            jax.ShapeDtypeStruct((1, 2 * layers * rec), jnp.float32),
        ],
        scratch_shapes=[
            pltpu.VMEM((len(pages), layers) + rows, fresh.dtype),
            pltpu.VMEM((2 * layers * rec, rows[-1]), jnp.float32),
            pltpu.SemaphoreType.DMA((len(flat),)),
        ],
        cost_estimate=FREE,
        compiler_params=PARAMS,
    )(starts, lengths, spots, *flat, fresh)


def make_local(n, tps):
    def shift(value, k):
        return lax.ppermute(value, "hold", [(i, (i + k) % n) for i in range(n)])

    def swap(value, axis, size, bit):
        return lax.ppermute(value, axis, [(i, i ^ bit) for i in range(size)])

    def local(cache_store, span_lengths, span_holder, rec_pos, hidden, norm_gain, kv_weight):
        me = lax.axis_index("hold")
        my_tp = lax.axis_index("tp")
        rec = hidden.shape[1]
        feats = kv_weight.shape[1]
        heads_here, head_size = kv_weight.shape[2], kv_weight.shape[4]
        cols = heads_here * 2 * head_size
        odds = sorted(range(1, n, 2), key=lambda k: min(k, n - k))
        evens = sorted(range(2, n, 2), key=lambda k: min(k, n - k))
        cuts = tps
        while feats % (cuts * 128):
            cuts //= 2
        part = feats // cuts
        share = my_tp % cuts

        own, *pieces = normed_shares(hidden, norm_gain, me, share, n, feats, part)
        arrived = {k: shift(pieces[k - 1], k) for k in odds + evens}
        at = [(me + k) % n for k in range(n)]
        names = [(k, None) for k in odds[::-1] + evens]
        picked = pick(cache_store, at, names + [(0, None)])
        there, last = {}, ()
        for name, page in zip(names, picked):
            there[name] = shift(tie(page, *last) if last else page, name[0])
            last = (there[name],)
        pages = [[picked[-1]]] + [[there[k, None]] for k in range(1, n)]

        weight = kv_weight.reshape(LAYERS, feats, cols)
        arrived[odds[0]] = tie(arrived[odds[0]], weight[:1, :8, :128])

        def everyone(piece):
            shares, masks, bit = [piece], [0], cuts // 2
            while bit:
                shares = shares + [swap(value, "tp", tps, bit) for value in shares]
                masks = masks + [mask ^ bit for mask in masks]
                bit //= 2
            return shares, [(share ^ mask) * part for mask in masks]

        even = me % 2 == 0
        half = n // 2
        blocks = [everyone(arrived[k]) for k in odds]
        order = [jnp.where(even, (k + 1) // 2 % half, (k - 1) // 2) for k in odds]
        away = products([a[0] for a in blocks], weight, order, [a[1] for a in blocks], rec)
        blocks = [everyone(arrived[k]) for k in range(2, n, 2)] + [([own], [jnp.int32(0)])]
        order = [jnp.int32(i) for i in range(half)]
        mine = products([a[0] for a in blocks], weight, order, [a[1] for a in blocks], rec)
        theirs = [swap(away[i % half], "hold", n, 1) for i in range(1, half + 1)]
        total = mine[-1] + theirs[-1]
        if n > 2:
            pairs = add_pairs(mine[:-1], theirs[:-1])
            for k, pair in zip(range(2, n, 2), pairs):
                total = total + shift(pair, -k)
        fresh = total.astype(jnp.bfloat16).reshape(LAYERS, rec, heads_here, 2, head_size)

        lengths = span_lengths[0]
        starts = jnp.cumsum(lengths) - lengths
        holders = (me - jnp.arange(n, dtype=jnp.int32)) % n
        held_here = span_holder[0][None, :] == holders[:, None]
        slot_starts = jnp.sum(jnp.where(held_here, starts[None, :], 0), axis=1)
        slot_lengths = jnp.sum(jnp.where(held_here, lengths[None, :], 0), axis=1)
        spots = (rec_pos - me * PROMPT_PER_HOLD).reshape(-1)
        united, sums = unite(pages, fresh, slot_starts, slot_lengths, spots)
        sums = lax.psum(sums, "tp").reshape(2, LAYERS, rec)
        entries = KVH * 2 * head_size
        deviation = sums[0] / entries / (sums[1] / entries + 1e-06)
        return (united, deviation)

    return local


def solution(mesh):
    return jax.shard_map(
        make_local(mesh.shape["hold"], mesh.shape["tp"]),
        mesh=mesh,
        in_specs=(
            P(None, ("groups", "hold"), None, "tp", None, None),
            P(("groups", "hold"), None),
            P(("groups", "hold"), None),
            P(None, ("groups", "hold")),
            P(None, ("groups", "hold"), None),
            P(),
            P(None, "hold", "tp", None, None),
        ),
        out_specs=(P(None, ("groups", "hold"), "tp", None, None), P(None, ("groups", "hold"))),
        check_vma=False,
    )
```

```python
import functools

import jax
import jax.numpy as jnp
from jax import lax
from jax.experimental import pallas as pl
from jax.experimental.pallas import tpu as pltpu
from jax.sharding import PartitionSpec as P

KVH = 8
PROMPT_PER_HOLD = 512
LAYERS = 2
CHUNK = 8
ROWS = 16
UNROLL = 8
CUTS = 3
VMEM_BYTES = 16 * 1024 * 1024
PARAMS = pltpu.CompilerParams(vmem_limit_bytes=VMEM_BYTES)
WIDE = pltpu.CompilerParams(vmem_limit_bytes=60 * 1024 * 1024)
ANY = pl.BlockSpec(memory_space=pl.ANY)
VMEM = pl.BlockSpec(memory_space=pltpu.VMEM)
SMEM = pl.BlockSpec(memory_space=pltpu.SMEM)


def norm_kernel(at, rows_ref, gain_ref, *outs):
    layers = gain_ref.shape[0]
    rec = rows_ref.shape[0] // layers
    columns = [pl.ds(pl.multiple_of(at[i], 128), out.shape[1]) for i, out in enumerate(outs)]
    for layer in range(layers):
        gains = [gain_ref[layer : layer + 1, column].astype(jnp.float32) for column in columns]

        def chunk(i, carry, layer=layer, gains=gains):
            here = pl.ds(pl.multiple_of(layer * rec + i * ROWS, ROWS), ROWS)
            rows = rows_ref[here, :].astype(jnp.float32)
            scale = lax.rsqrt(jnp.mean(rows * rows, axis=1, keepdims=True) + 1e-05)
            for out, column, gain in zip(outs, columns, gains):
                part = rows_ref[here, column].astype(jnp.float32)
                out[here, :] = (part * scale * gain).astype(jnp.bfloat16)
            return carry

        lax.fori_loop(0, rec // ROWS, chunk, 0)


def normed_shares(hidden, gain, me, share, n, feats, part):
    layers, rec, width = hidden.shape
    rows = layers * rec
    at = jnp.stack([me * feats] + [((me + k) % n) * feats + share * part for k in range(1, n)])
    sizes = [feats] + [part] * (n - 1)
    return pl.pallas_call(
        norm_kernel,
        in_specs=[SMEM, VMEM, VMEM],
        out_specs=[VMEM] * n,
        out_shape=[jax.ShapeDtypeStruct((rows, size), jnp.bfloat16) for size in sizes],
        compiler_params=PARAMS,
    )(at.astype(jnp.int32), hidden.reshape(rows, width), gain)


def tie_kernel(*refs):
    pass


def tie(value, *after):
    return pl.pallas_call(
        tie_kernel,
        in_specs=[ANY] * (1 + len(after)),
        out_specs=ANY,
        out_shape=jax.ShapeDtypeStruct(value.shape, value.dtype),
        input_output_aliases={0: 0},
        compiler_params=PARAMS,
    )(value, *after)


def pick_kernel(wanted, at, store, *refs):
    outs, held, sems = refs[: len(wanted)], refs[-2], refs[-1]
    moves = []
    for i, (out, (k, layer)) in enumerate(zip(outs, wanted)):
        for j in range(out.shape[0]):
            slot = len(moves)
            source = store.at[j if layer is None else layer, at[k]]
            fetch = pltpu.make_async_copy(source, held.at[slot], sems.at[0, slot])
            fetch.start()
            moves.append((fetch, pltpu.make_async_copy(held.at[slot], out.at[j], sems.at[1, slot])))
    for fetch, place in moves:
        fetch.wait()
        place.start()
    for _, place in moves:
        place.wait()


def pick(store, at, wanted):
    if not wanted:
        return []
    counts = [store.shape[0] if layer is None else 1 for _, layer in wanted]
    total = sum(counts)
    return pl.pallas_call(
        functools.partial(pick_kernel, wanted),
        grid_spec=pltpu.PrefetchScalarGridSpec(
            num_scalar_prefetch=1,
            grid=(),
            in_specs=[ANY],
            out_specs=[ANY] * len(wanted),
            scratch_shapes=[
                pltpu.VMEM((total,) + store.shape[2:], store.dtype),
                pltpu.SemaphoreType.DMA((2, total)),
            ],
        ),
        out_shape=[
            jax.ShapeDtypeStruct((count,) + store.shape[2:], store.dtype) for count in counts
        ],
        compiler_params=WIDE,
    )(jnp.stack(at).astype(jnp.int32), store)


def product_kernel(counts, at, *refs):
    weight, shares = refs[0], refs[1 : 1 + sum(counts)]
    held, loaded, sems, weight_sems = refs[-4:]
    outs = refs[-4 - len(counts) : -4]
    layers, rec, _ = outs[0].shape
    blocks = [i for i, count in enumerate(counts) for _ in range(count)]
    cuts = weight_sems.shape[1]
    chunk = weight.shape[1] // cuts
    placed, weights = [], []
    for layer in range(layers):
        placed.append([])
        for j, (share, i) in enumerate(zip(shares, blocks)):
            row = pl.ds(pl.multiple_of(at[i] * rec, 16), rec)
            column = pl.ds(pl.multiple_of(at[len(counts) + j], 128), share.shape[1])
            source, target = share.at[layer * rec : (layer + 1) * rec], held.at[layer, row, column]
            placed[layer].append(pltpu.make_async_copy(source, target, sems.at[j, layer]))
        weights.append([])
        for c in range(cuts):
            piece = pl.ds(c * chunk, chunk)
            source, target = weight.at[layer, piece], loaded.at[layer, piece]
            weights[layer].append(pltpu.make_async_copy(source, target, weight_sems.at[layer, c]))
        for copy in placed[layer] + weights[layer]:
            copy.start()
    for layer in range(layers):
        for copy in placed[layer]:
            copy.wait()
        total = None
        for c in range(cuts):
            weights[layer][c].wait()
            piece = slice(c * chunk, (c + 1) * chunk)
            result = jnp.dot(
                held[layer, :, piece], loaded[layer, piece], preferred_element_type=jnp.float32
            )
            total = result if total is None else total + result
        for i, out in enumerate(outs):
            out[layer] = total[i * rec : (i + 1) * rec]


def products(blocks, weight, order, columns, rec):
    counts = tuple(len(block) for block in blocks)
    at = jnp.stack(list(order) + [c for cs in columns for c in cs]).astype(jnp.int32)
    layers, feats, cols = weight.shape
    flat = [share for block in blocks for share in block]
    return pl.pallas_call(
        functools.partial(product_kernel, counts),
        in_specs=[SMEM] + [ANY] * (1 + len(flat)),
        out_specs=[VMEM] * len(blocks),
        out_shape=[jax.ShapeDtypeStruct((layers, rec, cols), jnp.float32)] * len(blocks),
        scratch_shapes=[
            pltpu.VMEM((layers, len(blocks) * rec, feats), jnp.bfloat16),
            pltpu.VMEM((layers, feats, cols), jnp.bfloat16),
            pltpu.SemaphoreType.DMA((len(flat), layers)),
            pltpu.SemaphoreType.DMA((layers, CUTS)),
        ],
        compiler_params=WIDE,
    )(at, weight, *flat)


def add_kernel(count, *refs):
    outs = refs[len(refs) - count :]
    for left, right, out in zip(refs[:count], refs[count : 2 * count], outs):
        out[...] = left[...] + right[...]


def add_pairs(left, right):
    count = len(left)
    return pl.pallas_call(
        functools.partial(add_kernel, count),
        in_specs=[VMEM] * (2 * count),
        out_specs=[VMEM] * count,
        out_shape=[jax.ShapeDtypeStruct(value.shape, value.dtype) for value in left],
        compiler_params=PARAMS,
    )(*left, *right)


def unite_kernel(counts, starts, lengths, spots, *refs):
    total = sum(counts)
    pages, (fresh, out, sums, held, squares, sems) = refs[:total], refs[total:]
    layers, rec = fresh.shape[:2]
    copies, base = [], 0
    for slot, count in enumerate(counts):
        copies.append([])
        for i in range(count):
            target = held.at[slot] if count == 1 else held.at[slot, pl.ds(i, 1)]
            copies[-1].append(pltpu.make_async_copy(pages[base + i], target, sems.at[base + i]))
            copies[-1][-1].start()
        base += count
    for slot in range(len(counts)):
        for copy in copies[slot]:
            copy.wait()
        start, length = starts[slot], lengths[slot]
        whole = length // CHUNK

        def many(i, carry, slot=slot, start=start):
            for layer in range(layers):
                out[layer, pl.ds(start + i * CHUNK, CHUNK)] = held[
                    slot, layer, pl.ds(i * CHUNK, CHUNK)
                ]
            return carry

        def one(i, carry, slot=slot, start=start):
            for layer in range(layers):
                out[layer, start + i] = held[slot, layer, i]
            return carry

        lax.fori_loop(0, whole, many, 0)
        lax.fori_loop(whole * CHUNK, length, one, 0)
    for layer in range(layers):

        def renew(j, carry, layer=layer):
            at = layer * rec + j
            spot = spots[at]
            old = out[layer, spot].astype(jnp.float32)
            new = fresh[layer, j]
            diff = new.astype(jnp.float32) - old
            squares[pl.ds(at, 1), :] = jnp.sum(jnp.sum(diff * diff, axis=0), axis=0, keepdims=True)
            squares[pl.ds(layers * rec + at, 1), :] = jnp.sum(
                jnp.sum(old * old, axis=0), axis=0, keepdims=True
            )
            out[layer, spot] = new
            return carry

        lax.fori_loop(0, rec, renew, 0, unroll=UNROLL)
    ones = jnp.ones((8, squares.shape[1]), jnp.float32)
    both = lax.dot_general(
        ones,
        squares[...],
        (((1,), (1,)), ((), ())),
        precision=lax.Precision.HIGHEST,
        preferred_element_type=jnp.float32,
    )
    sums[...] = both[0:1]


def unite(pages, fresh, starts, lengths, spots):
    counts = tuple(len(page) for page in pages)
    flat = [piece for page in pages for piece in page]
    layers, rec = fresh.shape[:2]
    rows = flat[0].shape[1:]
    return pl.pallas_call(
        functools.partial(unite_kernel, counts),
        in_specs=[SMEM] * 3 + [ANY] * len(flat) + [VMEM],
        out_specs=[VMEM, VMEM],
        out_shape=[
            jax.ShapeDtypeStruct((layers, PROMPT_PER_HOLD) + rows[1:], fresh.dtype),
            jax.ShapeDtypeStruct((1, 2 * layers * rec), jnp.float32),
        ],
        scratch_shapes=[
            pltpu.VMEM((len(pages), layers) + rows, fresh.dtype),
            pltpu.VMEM((2 * layers * rec, rows[-1]), jnp.float32),
            pltpu.SemaphoreType.DMA((len(flat),)),
        ],
        compiler_params=PARAMS,
    )(starts, lengths, spots, *flat, fresh)


def make_local(n, tps):
    def shift(value, k):
        return lax.ppermute(value, "hold", [(i, (i + k) % n) for i in range(n)])

    def swap(value, axis, size, bit):
        return lax.ppermute(value, axis, [(i, i ^ bit) for i in range(size)])

    def local(cache_store, span_lengths, span_holder, rec_pos, hidden, norm_gain, kv_weight):
        me = lax.axis_index("hold")
        my_tp = lax.axis_index("tp")
        rec = hidden.shape[1]
        feats = kv_weight.shape[1]
        heads_here, head_size = kv_weight.shape[2], kv_weight.shape[4]
        cols = heads_here * 2 * head_size
        odds = sorted(range(1, n, 2), key=lambda k: min(k, n - k))
        evens = sorted(range(2, n, 2), key=lambda k: min(k, n - k))
        cuts = tps
        while feats % (cuts * 128):
            cuts //= 2
        part = feats // cuts
        share = my_tp % cuts

        own, *pieces = normed_shares(hidden, norm_gain, me, share, n, feats, part)
        arrived = {k: shift(pieces[k - 1], k) for k in odds + evens}
        at = [(me + k) % n for k in range(n)]
        names = [(k, None) for k in odds[::-1] + evens]
        picked = pick(cache_store, at, names + [(0, None)])
        there, last = {}, ()
        for name, page in zip(names, picked):
            there[name] = shift(tie(page, *last) if last else page, name[0])
            last = (there[name],)
        pages = [[picked[-1]]] + [[there[k, None]] for k in range(1, n)]

        weight = kv_weight.reshape(LAYERS, feats, cols)
        arrived[odds[0]] = tie(arrived[odds[0]], weight[:1, :8, :128])

        def everyone(piece):
            shares, masks, bit = [piece], [0], cuts // 2
            while bit:
                shares = shares + [swap(value, "tp", tps, bit) for value in shares]
                masks = masks + [mask ^ bit for mask in masks]
                bit //= 2
            return shares, [(share ^ mask) * part for mask in masks]

        even = me % 2 == 0
        half = n // 2
        blocks = [everyone(arrived[k]) for k in odds]
        order = [jnp.where(even, (k + 1) // 2 % half, (k - 1) // 2) for k in odds]
        away = products([a[0] for a in blocks], weight, order, [a[1] for a in blocks], rec)
        blocks = [everyone(arrived[k]) for k in range(2, n, 2)] + [([own], [jnp.int32(0)])]
        order = [jnp.int32(i) for i in range(half)]
        mine = products([a[0] for a in blocks], weight, order, [a[1] for a in blocks], rec)
        theirs = [swap(away[i % half], "hold", n, 1) for i in range(1, half + 1)]
        total = mine[-1] + theirs[-1]
        if n > 2:
            pairs = add_pairs(mine[:-1], theirs[:-1])
            for k, pair in zip(range(2, n, 2), pairs):
                total = total + shift(pair, -k)
        fresh = total.astype(jnp.bfloat16).reshape(LAYERS, rec, heads_here, 2, head_size)

        lengths = span_lengths[0]
        starts = jnp.cumsum(lengths) - lengths
        holders = (me - jnp.arange(n, dtype=jnp.int32)) % n
        held_here = span_holder[0][None, :] == holders[:, None]
        slot_starts = jnp.sum(jnp.where(held_here, starts[None, :], 0), axis=1)
        slot_lengths = jnp.sum(jnp.where(held_here, lengths[None, :], 0), axis=1)
        spots = (rec_pos - me * PROMPT_PER_HOLD).reshape(-1)
        united, sums = unite(pages, fresh, slot_starts, slot_lengths, spots)
        sums = lax.psum(sums, "tp").reshape(2, LAYERS, rec)
        entries = KVH * 2 * head_size
        deviation = sums[0] / entries / (sums[1] / entries + 1e-06)
        return (united, deviation)

    return local


def solution(mesh):
    return jax.shard_map(
        make_local(mesh.shape["hold"], mesh.shape["tp"]),
        mesh=mesh,
        in_specs=(
            P(None, ("groups", "hold"), None, "tp", None, None),
            P(("groups", "hold"), None),
            P(("groups", "hold"), None),
            P(None, ("groups", "hold")),
            P(None, ("groups", "hold"), None),
            P(),
            P(None, "hold", "tp", None, None),
        ),
        out_specs=(P(None, ("groups", "hold"), "tp", None, None), P(None, ("groups", "hold"))),
        check_vma=False,
    )
```

```python
import functools

import jax
import jax.numpy as jnp
from jax import lax
from jax.experimental import pallas as pl
from jax.experimental.pallas import tpu as pltpu
from jax.sharding import PartitionSpec as P

KVH = 8
PROMPT_PER_HOLD = 512
LAYERS = 2
CHUNK = 8
ROWS = 16
UNROLL = 20
CUTS = 3
VMEM_BYTES = 16 * 1024 * 1024
PARAMS = pltpu.CompilerParams(vmem_limit_bytes=VMEM_BYTES)
WIDE = pltpu.CompilerParams(vmem_limit_bytes=60 * 1024 * 1024)
ANY = pl.BlockSpec(memory_space=pl.ANY)
VMEM = pl.BlockSpec(memory_space=pltpu.VMEM)
SMEM = pl.BlockSpec(memory_space=pltpu.SMEM)


def norm_kernel(at, rows_ref, gain_ref, *outs):
    layers = gain_ref.shape[0]
    rec = rows_ref.shape[0] // layers
    columns = [pl.ds(pl.multiple_of(at[i], 128), out.shape[1]) for i, out in enumerate(outs)]
    for layer in range(layers):
        gains = [gain_ref[layer : layer + 1, column].astype(jnp.float32) for column in columns]

        def chunk(i, carry, layer=layer, gains=gains):
            here = pl.ds(pl.multiple_of(layer * rec + i * ROWS, ROWS), ROWS)
            rows = rows_ref[here, :].astype(jnp.float32)
            scale = lax.rsqrt(jnp.mean(rows * rows, axis=1, keepdims=True) + 1e-05)
            for out, column, gain in zip(outs, columns, gains):
                part = rows_ref[here, column].astype(jnp.float32)
                out[here, :] = (part * scale * gain).astype(jnp.bfloat16)
            return carry

        lax.fori_loop(0, rec // ROWS, chunk, 0)


def normed_shares(hidden, gain, me, share, n, feats, part):
    layers, rec, width = hidden.shape
    rows = layers * rec
    at = jnp.stack([me * feats] + [((me + k) % n) * feats + share * part for k in range(1, n)])
    sizes = [feats] + [part] * (n - 1)
    return pl.pallas_call(
        norm_kernel,
        in_specs=[SMEM, VMEM, VMEM],
        out_specs=[VMEM] * n,
        out_shape=[jax.ShapeDtypeStruct((rows, size), jnp.bfloat16) for size in sizes],
        compiler_params=PARAMS,
    )(at.astype(jnp.int32), hidden.reshape(rows, width), gain)


def tie_kernel(*refs):
    pass


def tie(value, *after):
    return pl.pallas_call(
        tie_kernel,
        in_specs=[ANY] * (1 + len(after)),
        out_specs=ANY,
        out_shape=jax.ShapeDtypeStruct(value.shape, value.dtype),
        input_output_aliases={0: 0},
        compiler_params=PARAMS,
    )(value, *after)


def pick_kernel(wanted, at, store, *refs):
    outs, held, sems = refs[: len(wanted)], refs[-2], refs[-1]
    moves = []
    for i, (out, (k, layer)) in enumerate(zip(outs, wanted)):
        for j in range(out.shape[0]):
            slot = len(moves)
            source = store.at[j if layer is None else layer, at[k]]
            fetch = pltpu.make_async_copy(source, held.at[slot], sems.at[0, slot])
            fetch.start()
            moves.append((fetch, pltpu.make_async_copy(held.at[slot], out.at[j], sems.at[1, slot])))
    for fetch, place in moves:
        fetch.wait()
        place.start()
    for _, place in moves:
        place.wait()


def pick(store, at, wanted):
    if not wanted:
        return []
    counts = [store.shape[0] if layer is None else 1 for _, layer in wanted]
    total = sum(counts)
    return pl.pallas_call(
        functools.partial(pick_kernel, wanted),
        grid_spec=pltpu.PrefetchScalarGridSpec(
            num_scalar_prefetch=1,
            grid=(),
            in_specs=[ANY],
            out_specs=[ANY] * len(wanted),
            scratch_shapes=[
                pltpu.VMEM((total,) + store.shape[2:], store.dtype),
                pltpu.SemaphoreType.DMA((2, total)),
            ],
        ),
        out_shape=[
            jax.ShapeDtypeStruct((count,) + store.shape[2:], store.dtype) for count in counts
        ],
        compiler_params=WIDE,
    )(jnp.stack(at).astype(jnp.int32), store)


def product_kernel(counts, at, *refs):
    weight, shares = refs[0], refs[1 : 1 + sum(counts)]
    held, loaded, sems, weight_sems = refs[-4:]
    outs = refs[-4 - len(counts) : -4]
    layers, rec, _ = outs[0].shape
    blocks = [i for i, count in enumerate(counts) for _ in range(count)]
    cuts = weight_sems.shape[1]
    chunk = weight.shape[1] // cuts
    placed, weights = [], []
    for layer in range(layers):
        placed.append([])
        for j, (share, i) in enumerate(zip(shares, blocks)):
            row = pl.ds(pl.multiple_of(at[i] * rec, 16), rec)
            column = pl.ds(pl.multiple_of(at[len(counts) + j], 128), share.shape[1])
            source, target = share.at[layer * rec : (layer + 1) * rec], held.at[layer, row, column]
            placed[layer].append(pltpu.make_async_copy(source, target, sems.at[j, layer]))
        weights.append([])
        for c in range(cuts):
            piece = pl.ds(c * chunk, chunk)
            source, target = weight.at[layer, piece], loaded.at[layer, piece]
            weights[layer].append(pltpu.make_async_copy(source, target, weight_sems.at[layer, c]))
        for copy in placed[layer] + weights[layer]:
            copy.start()
    for layer in range(layers):
        for copy in placed[layer]:
            copy.wait()
        total = None
        for c in range(cuts):
            weights[layer][c].wait()
            piece = slice(c * chunk, (c + 1) * chunk)
            result = jnp.dot(
                held[layer, :, piece], loaded[layer, piece], preferred_element_type=jnp.float32
            )
            total = result if total is None else total + result
        for i, out in enumerate(outs):
            out[layer] = total[i * rec : (i + 1) * rec]


def products(blocks, weight, order, columns, rec):
    counts = tuple(len(block) for block in blocks)
    at = jnp.stack(list(order) + [c for cs in columns for c in cs]).astype(jnp.int32)
    layers, feats, cols = weight.shape
    flat = [share for block in blocks for share in block]
    return pl.pallas_call(
        functools.partial(product_kernel, counts),
        in_specs=[SMEM] + [ANY] * (1 + len(flat)),
        out_specs=[VMEM] * len(blocks),
        out_shape=[jax.ShapeDtypeStruct((layers, rec, cols), jnp.float32)] * len(blocks),
        scratch_shapes=[
            pltpu.VMEM((layers, len(blocks) * rec, feats), jnp.bfloat16),
            pltpu.VMEM((layers, feats, cols), jnp.bfloat16),
            pltpu.SemaphoreType.DMA((len(flat), layers)),
            pltpu.SemaphoreType.DMA((layers, CUTS)),
        ],
        compiler_params=WIDE,
    )(at, weight, *flat)


def add_kernel(count, *refs):
    outs = refs[len(refs) - count :]
    for left, right, out in zip(refs[:count], refs[count : 2 * count], outs):
        out[...] = left[...] + right[...]


def add_pairs(left, right):
    count = len(left)
    return pl.pallas_call(
        functools.partial(add_kernel, count),
        in_specs=[VMEM] * (2 * count),
        out_specs=[VMEM] * count,
        out_shape=[jax.ShapeDtypeStruct(value.shape, value.dtype) for value in left],
        compiler_params=PARAMS,
    )(*left, *right)


def unite_kernel(counts, starts, lengths, spots, *refs):
    total = sum(counts)
    pages, (fresh, out, sums, held, squares, sems) = refs[:total], refs[total:]
    layers, rec = fresh.shape[:2]
    copies, base = [], 0
    for slot, count in enumerate(counts):
        copies.append([])
        for i in range(count):
            target = held.at[slot] if count == 1 else held.at[slot, pl.ds(i, 1)]
            copies[-1].append(pltpu.make_async_copy(pages[base + i], target, sems.at[base + i]))
            copies[-1][-1].start()
        base += count
    for slot in range(len(counts)):
        for copy in copies[slot]:
            copy.wait()
        start, length = starts[slot], lengths[slot]
        whole = length // CHUNK

        def many(i, carry, slot=slot, start=start):
            for layer in range(layers):
                out[layer, pl.ds(start + i * CHUNK, CHUNK)] = held[
                    slot, layer, pl.ds(i * CHUNK, CHUNK)
                ]
            return carry

        def one(i, carry, slot=slot, start=start):
            for layer in range(layers):
                out[layer, start + i] = held[slot, layer, i]
            return carry

        lax.fori_loop(0, whole, many, 0)
        lax.fori_loop(whole * CHUNK, length, one, 0)
    for layer in range(layers):

        def renew(j, carry, layer=layer):
            at = layer * rec + j
            spot = spots[at]
            old = out[layer, spot].astype(jnp.float32)
            new = fresh[layer, j]
            diff = new.astype(jnp.float32) - old
            squares[pl.ds(at, 1), :] = jnp.sum(jnp.sum(diff * diff, axis=0), axis=0, keepdims=True)
            squares[pl.ds(layers * rec + at, 1), :] = jnp.sum(
                jnp.sum(old * old, axis=0), axis=0, keepdims=True
            )
            out[layer, spot] = new
            return carry

        lax.fori_loop(0, rec, renew, 0, unroll=UNROLL)
    ones = jnp.ones((8, squares.shape[1]), jnp.float32)
    both = lax.dot_general(
        ones,
        squares[...],
        (((1,), (1,)), ((), ())),
        precision=lax.Precision.HIGHEST,
        preferred_element_type=jnp.float32,
    )
    sums[...] = both[0:1]


def unite(pages, fresh, starts, lengths, spots):
    counts = tuple(len(page) for page in pages)
    flat = [piece for page in pages for piece in page]
    layers, rec = fresh.shape[:2]
    rows = flat[0].shape[1:]
    return pl.pallas_call(
        functools.partial(unite_kernel, counts),
        in_specs=[SMEM] * 3 + [ANY] * len(flat) + [VMEM],
        out_specs=[VMEM, VMEM],
        out_shape=[
            jax.ShapeDtypeStruct((layers, PROMPT_PER_HOLD) + rows[1:], fresh.dtype),
            jax.ShapeDtypeStruct((1, 2 * layers * rec), jnp.float32),
        ],
        scratch_shapes=[
            pltpu.VMEM((len(pages), layers) + rows, fresh.dtype),
            pltpu.VMEM((2 * layers * rec, rows[-1]), jnp.float32),
            pltpu.SemaphoreType.DMA((len(flat),)),
        ],
        compiler_params=PARAMS,
    )(starts, lengths, spots, *flat, fresh)


def make_local(n, tps):
    def shift(value, k):
        return lax.ppermute(value, "hold", [(i, (i + k) % n) for i in range(n)])

    def swap(value, axis, size, bit):
        return lax.ppermute(value, axis, [(i, i ^ bit) for i in range(size)])

    def local(cache_store, span_lengths, span_holder, rec_pos, hidden, norm_gain, kv_weight):
        me = lax.axis_index("hold")
        my_tp = lax.axis_index("tp")
        rec = hidden.shape[1]
        feats = kv_weight.shape[1]
        heads_here, head_size = kv_weight.shape[2], kv_weight.shape[4]
        cols = heads_here * 2 * head_size
        odds = sorted(range(1, n, 2), key=lambda k: min(k, n - k))
        evens = sorted(range(2, n, 2), key=lambda k: min(k, n - k))
        cuts = tps
        while feats % (cuts * 128):
            cuts //= 2
        part = feats // cuts
        share = my_tp % cuts

        own, *pieces = normed_shares(hidden, norm_gain, me, share, n, feats, part)
        arrived = {k: shift(pieces[k - 1], k) for k in odds + evens}
        at = [(me + k) % n for k in range(n)]
        names = [(k, None) for k in odds[::-1] + evens]
        picked = pick(cache_store, at, names + [(0, None)])
        there, last = {}, ()
        for name, page in zip(names, picked):
            there[name] = shift(tie(page, *last) if last else page, name[0])
            last = (there[name],)
        pages = [[picked[-1]]] + [[there[k, None]] for k in range(1, n)]

        weight = kv_weight.reshape(LAYERS, feats, cols)
        arrived[odds[0]] = tie(arrived[odds[0]], weight[:1, :8, :128])

        def everyone(piece):
            shares, masks, bit = [piece], [0], cuts // 2
            while bit:
                shares = shares + [swap(value, "tp", tps, bit) for value in shares]
                masks = masks + [mask ^ bit for mask in masks]
                bit //= 2
            return shares, [(share ^ mask) * part for mask in masks]

        even = me % 2 == 0
        half = n // 2
        blocks = [everyone(arrived[k]) for k in odds]
        order = [jnp.where(even, (k + 1) // 2 % half, (k - 1) // 2) for k in odds]
        away = products([a[0] for a in blocks], weight, order, [a[1] for a in blocks], rec)
        blocks = [everyone(arrived[k]) for k in range(2, n, 2)] + [([own], [jnp.int32(0)])]
        order = [jnp.int32(i) for i in range(half)]
        mine = products([a[0] for a in blocks], weight, order, [a[1] for a in blocks], rec)
        theirs = [swap(away[i % half], "hold", n, 1) for i in range(1, half + 1)]
        total = mine[-1] + theirs[-1]
        if n > 2:
            pairs = add_pairs(mine[:-1], theirs[:-1])
            for k, pair in zip(range(2, n, 2), pairs):
                total = total + shift(pair, -k)
        fresh = total.astype(jnp.bfloat16).reshape(LAYERS, rec, heads_here, 2, head_size)

        lengths = span_lengths[0]
        starts = jnp.cumsum(lengths) - lengths
        holders = (me - jnp.arange(n, dtype=jnp.int32)) % n
        held_here = span_holder[0][None, :] == holders[:, None]
        slot_starts = jnp.sum(jnp.where(held_here, starts[None, :], 0), axis=1)
        slot_lengths = jnp.sum(jnp.where(held_here, lengths[None, :], 0), axis=1)
        spots = (rec_pos - me * PROMPT_PER_HOLD).reshape(-1)
        united, sums = unite(pages, fresh, slot_starts, slot_lengths, spots)
        sums = lax.psum(sums, "tp").reshape(2, LAYERS, rec)
        entries = KVH * 2 * head_size
        deviation = sums[0] / entries / (sums[1] / entries + 1e-06)
        return (united, deviation)

    return local


def solution(mesh):
    return jax.shard_map(
        make_local(mesh.shape["hold"], mesh.shape["tp"]),
        mesh=mesh,
        in_specs=(
            P(None, ("groups", "hold"), None, "tp", None, None),
            P(("groups", "hold"), None),
            P(("groups", "hold"), None),
            P(None, ("groups", "hold")),
            P(None, ("groups", "hold"), None),
            P(),
            P(None, "hold", "tp", None, None),
        ),
        out_specs=(P(None, ("groups", "hold"), "tp", None, None), P(None, ("groups", "hold"))),
        check_vma=False,
    )
```
